512 devices in a mesh: shot: 8 (over x, core), brick: 64 (over z, y).
Axes of the slice: x: 4, y: 4, z: 16, core: 2. Of those that a mesh axis runs over, the one named last changes fastest.
Arguments:
- adjoint_prev: float32 [16, 512, 64, 256], P('shot', 'brick'), may hold values from -6 to 6
- adjoint_now: float32 [16, 512, 64, 256], P('shot', 'brick'), may hold values from -6 to 6
- forward_snaps: bfloat16 [16, 2, 512, 64, 256], P('shot', None, 'brick'), may hold values from -6 to 6
- courant: float32 [512, 64, 256], P('brick'), may hold values from 0.05 to 0.2
- traces: float32 [16, 2, 256], P('shot'), may hold values from -12 to 12
- rec_x: int32 [16, 256], P('shot'), may hold values from 0 to 511
- rec_y: int32 [16, 256], P('shot'), may hold values from 0 to 255
- water_rows: int32 [512, 256], P('brick'), may hold values from 0 to 16
- direction: float32 [512, 64, 256], P('brick'), may hold values from -6 to 6
Outputs:
- gradient: float32 [512, 64, 256], P('brick', 'shot')
- step_sums: float32 [2], replicated
The draws below stay inside these ranges and needn't reach their ends.
All inputs are finite; a program needn't handle non-finite values.
Results may differ from the reference program's by a relative error of at most 0.002.
Values sent between devices are 32-bit elements; how exact they have to be, the bound alone decides.
No kernel may reach another device: no remote copies, remote signals or barrier semaphores. Data moves between devices by JAX's collectives and lax.ppermute only.
A program may use at most 64 MiB of HBM per device.

```python
import jax
import jax.numpy as jnp
from jax import lax

NY = 256
NZ = 64
NREC = 256
NX = 512
SHOTS = 16


def plant(entries, rng, low, top_value):
    longest = entries.shape.index(max(entries.shape))
    spots = []
    for shift in (0, 1):
        where = [jax.random.randint(jax.random.fold_in(rng, axis), (), 0, length) for axis, length in enumerate(entries.shape)]
        where[longest] = (where[longest] + shift) % entries.shape[longest]
        spots.append(tuple(where))
    return entries.at[spots[0]].set(low).at[spots[1]].set(top_value)


def levels(rng, shape, shards, smallest, high):
    loudness = 1.0
    for dim, parts in shards:
        heights = jax.random.uniform(jax.random.fold_in(jax.random.fold_in(rng, 6), dim), (parts,), jnp.float32, smallest / len(shards), high / len(shards))
        loudness = loudness * jnp.repeat(jnp.exp(heights), shape[dim] // parts).reshape((-1,) + (1,) * (len(shape) - 1 - dim))
    return loudness


def noise(key, shape, scale, most, cuts=(), kind=jnp.bfloat16):
    entries = scale * jax.random.normal(key, shape, jnp.float32)
    if cuts:
        entries = entries * levels(key, shape, cuts, -0.22, 0.18)
    return jnp.clip(entries, -most, most).astype(kind)


def setup_inputs(seed: int = 0) -> dict:
    arg_keys = jax.random.split(jax.random.key(seed), 10)
    return {
        "adjoint_prev": noise(arg_keys[0], (SHOTS, NX, NZ, NY), 1.0, 6.0, ((0, 8), (1, 64)), jnp.float32),
        "adjoint_now": noise(arg_keys[1], (SHOTS, NX, NZ, NY), 1.0, 6.0, ((0, 8), (1, 64)), jnp.float32),
        "forward_snaps": noise(arg_keys[2], (SHOTS, 2, NX, NZ, NY), 1.0, 6.0, ((0, 8), (2, 64))),
        "courant": jnp.clip(0.05 + 0.15 * jax.random.uniform(arg_keys[3], (NX, NZ, NY), jnp.float32) ** levels(arg_keys[3], (NX, NZ, NY), ((0, 64),), -0.2, 0.2), 0.05, 0.2),
        "traces": noise(arg_keys[4], (SHOTS, 2, NREC), 2.0, 12.0, ((0, 8),), jnp.float32),
        "rec_x": plant(jax.random.randint(arg_keys[5], (SHOTS, NREC), 0, NX), jax.random.fold_in(arg_keys[5], 1), 0, NX - 1).astype(jnp.int32),
        "rec_y": plant(jax.random.randint(arg_keys[6], (SHOTS, NREC), 0, NY), jax.random.fold_in(arg_keys[6], 1), 0, NY - 1).astype(jnp.int32),
        "water_rows": plant(jax.random.randint(arg_keys[7], (NX, NY), 0, NZ // 4 + 1), jax.random.fold_in(arg_keys[7], 1), 0, (NZ // 4 + 1) - 1).astype(jnp.int32),
        "direction": noise(arg_keys[8], (NX, NZ, NY), 1.0, 6.0, ((0, 64),), jnp.float32),
    }


far_coef = -1.0 / 12.0
near_coef = 4.0 / 3.0
center_coef = -2.5
receiver_depth = 2
water_level = 0.1


def laplace(ext):
    inner = ext[..., 2:-2, :, :]
    along_x = far_coef * (ext[..., 0:-4, :, :] + ext[..., 4:, :, :]) + near_coef * (ext[..., 1:-3, :, :] + ext[..., 3:-1, :, :])
    widths = [(0, 0)] * (inner.ndim - 2) + [(2, 2), (2, 2)]
    padded = jnp.pad(inner, widths)
    along_z = far_coef * (padded[..., 0:-4, 2:-2] + padded[..., 4:, 2:-2]) + near_coef * (padded[..., 1:-3, 2:-2] + padded[..., 3:-1, 2:-2])
    along_y = far_coef * (padded[..., 2:-2, 0:-4] + padded[..., 2:-2, 4:]) + near_coef * (padded[..., 2:-2, 1:-3] + padded[..., 2:-2, 3:-1])
    return along_x + along_z + along_y + 3.0 * center_coef * inner


def reference(adjoint_prev, adjoint_now, forward_snaps, courant, traces, rec_x, rec_y, water_rows, direction):
    def one_shot(carry, items):
        image, illum = carry
        prev, now, snaps, trace, row_x, row_y = items
        inject0 = jnp.zeros((NX, NZ, NY), jnp.float32).at[row_x, receiver_depth, row_y].add(trace[0])
        inject1 = jnp.zeros((NX, NZ, NY), jnp.float32).at[row_x, receiver_depth, row_y].add(trace[1])
        padding = ((2, 2), (0, 0), (0, 0))
        first = 2.0 * now - prev + courant * laplace(jnp.pad(now, padding)) + inject0
        second = 2.0 * first - now + courant * laplace(jnp.pad(first, padding)) + inject1
        snap0 = snaps[0].astype(jnp.float32)
        snap1 = snaps[1].astype(jnp.float32)
        image = image + (snap0 * first + snap1 * second)
        illum = illum + (snap0 * snap0 + snap1 * snap1)
        return (image, illum), None

    zeros = jnp.zeros((NX, NZ, NY), jnp.float32)
    (image, illum), _ = lax.scan(one_shot, (zeros, zeros), (adjoint_prev, adjoint_now, forward_snaps, traces, rec_x, rec_y))
    peak = jnp.max(illum)
    depth = jnp.arange(NZ, dtype=jnp.int32)
    keep = depth[None, :, None] >= water_rows[:, None, :]
    gradient = jnp.where(keep, image / (illum + water_level * peak), jnp.float32(0.0))
    step_sums = jnp.stack([jnp.sum(gradient * gradient), jnp.sum(gradient * direction)])
    return gradient, step_sums
```

```python
import functools

import jax
import jax.numpy as jnp
from jax import lax
from jax.experimental import pallas as pl
from jax.experimental.pallas import tpu as pltpu
from jax.sharding import PartitionSpec as P

far_coef = -1.0 / 12.0
near_coef = 4.0 / 3.0
receiver_depth = 2
water_level = 0.1
f32 = jnp.float32
bf16 = jnp.bfloat16


def vmem(count):
    return [pl.BlockSpec(memory_space=pltpu.VMEM)] * count


mib = 1024 * 1024
params = pltpu.CompilerParams(vmem_limit_bytes=16 * mib)


def band(size, center):
    gap = jnp.abs(
        lax.broadcasted_iota(jnp.int32, (size, size), 0)
        - lax.broadcasted_iota(jnp.int32, (size, size), 1)
    )
    weights = jnp.where(gap == 0, f32(center), f32(0.0))
    weights = jnp.where(gap == 1, f32(16.0), weights)
    return jnp.where(gap == 2, f32(-1.0), weights).astype(bf16)


def split_two(v):
    high = v.astype(bf16)
    return high, (v - high.astype(f32)).astype(bf16)


def in_plane(v, band_z, band_y):
    high, low = split_two(v)
    out = jnp.dot(band_z, high, preferred_element_type=f32)
    out += jnp.dot(band_z, low, preferred_element_type=f32)
    out += jnp.dot(high, band_y, preferred_element_type=f32)
    out += jnp.dot(low, band_y, preferred_element_type=f32)
    return out


def injected(trace, row_x, row_y, first_row, rows, cells_y):
    receivers = trace.shape[1]
    at_x = row_x == first_row + lax.broadcasted_iota(jnp.int32, (rows, receivers), 0)
    at_y = (row_y == lax.broadcasted_iota(jnp.int32, (cells_y, receivers), 0)).astype(f32)
    at_y = at_y.astype(bf16)
    rest = jnp.where(at_x, trace, f32(0.0))
    out = jnp.zeros((rows, cells_y), f32)
    for _ in range(3):
        part = rest.astype(bf16)
        rest = rest - part.astype(f32)
        out += lax.dot_general(
            part, at_y, (((1,), (1,)), ((), ())), preferred_element_type=f32
        )
    return out


def illum_kernel(snaps, core, out):
    shots, steps, planes, depth, width = snaps.shape
    parts = 2 * out.shape[1]
    rows = depth // parts
    mine = core[0]
    for i in range(planes):
        total = None
        for s in range(shots):
            for k in range(steps):
                v = snaps[s, k, i].astype(f32)
                total = v * v if total is None else total + v * v
        for p in range(parts):
            slot = (mine + p % 2) % 2
            out[slot, p // 2, i] = total[p * rows : (p + 1) * rows]


def local_kernel(
    prev, now, courant, traces, rec_x, rec_y, first_row, order, out, head, tail, plane
):
    shots, planes, depth, width = now.shape
    band_y = band(width, -90.0)
    band_z = band(depth, 0.0)
    for s in range(shots):
        plane[...] = injected(
            traces[s, 0:1], rec_x[s : s + 1], rec_y[s : s + 1], first_row[0], planes, width
        )
        for i in range(planes):
            v = now[s, i]
            total = in_plane(v, band_z, band_y)
            for gap, weight in ((1, 16.0), (2, -1.0)):
                for j in (i - gap, i + gap):
                    if 0 <= j < planes:
                        total += weight * now[s, j]
            out[s, i] = 2.0 * v - prev[s, i] + courant[i] * (total * (1.0 / 12.0))
            out[s, i, receiver_depth : receiver_depth + 1] += plane[i : i + 1]
        for j in range(2):
            head[s, j] = out[s, j]
            tail[s, j] = out[s, planes - 2 + j]
            head[shots + s, j] = now[s, j]
            tail[shots + s, j] = now[s, planes - 2 + j]
    for j in range(2):
        head[2 * shots, j] = courant[j]
        tail[2 * shots, j] = courant[planes - 2 + j]


def image_kernel(
    local, now, courant, before, after, snaps,
    traces, rec_x, rec_y, first_row, core, order, out, first, plane,
):
    shots, planes, depth, width = now.shape
    parts = 2 * out.shape[1]
    rows = depth // parts
    band_y = band(width, -90.0)
    band_z = band(depth, 0.0)
    mine = core[0]
    last = planes - 1
    for s in range(shots):
        first[s, 2] = local[s, 0] + courant[0] * (
            far_coef * before[shots + s, 0] + near_coef * before[shots + s, 1]
        )
        first[s, 3] = local[s, 1] + courant[1] * (far_coef * before[shots + s, 1])
        for i in range(2, planes - 2):
            first[s, i + 2] = local[s, i]
        first[s, planes] = local[s, last - 1] + courant[last - 1] * (far_coef * after[shots + s, 0])
        first[s, planes + 1] = local[s, last] + courant[last] * (
            near_coef * after[shots + s, 0] + far_coef * after[shots + s, 1]
        )
        first[s, 0] = before[s, 0] + before[2 * shots, 0] * (far_coef * now[s, 0])
        first[s, 1] = before[s, 1] + before[2 * shots, 1] * (
            near_coef * now[s, 0] + far_coef * now[s, 1]
        )
        first[s, planes + 2] = after[s, 0] + after[2 * shots, 0] * (
            near_coef * now[s, last] + far_coef * now[s, last - 1]
        )
        first[s, planes + 3] = after[s, 1] + after[2 * shots, 1] * (far_coef * now[s, last])
        plane[s] = injected(
            traces[s, 1:2], rec_x[s : s + 1], rec_y[s : s + 1], first_row[0], planes, width
        )
    at_level = (
        lax.broadcasted_iota(jnp.int32, (depth, width), 0) == receiver_depth
    )
    for i in range(planes):
        image = None
        for s in range(shots):
            v = first[s, i + 2]
            total = in_plane(v, band_z, band_y)
            total += 16.0 * (first[s, i + 1] + first[s, i + 3])
            total -= first[s, i] + first[s, i + 4]
            second = 2.0 * v - now[s, i] + courant[i] * (total * (1.0 / 12.0))
            second += jnp.where(at_level, plane[s, i : i + 1], f32(0.0))
            term = snaps[s, 0, i].astype(f32) * v + snaps[s, 1, i].astype(f32) * second
            image = term if image is None else image + term
        for p in range(parts):
            slot = (mine + p % 2) % 2
            out[slot, p // 2, i] = image[p * rows : (p + 1) * rows]


def folded(line, combine):
    out = line[:, :128]
    for j in range(128, line.shape[1], 128):
        out = combine(out, line[:, j : j + 128])
    return out


def peak_kernel(got, part, peak):
    total = got[0]
    for c in range(1, got.shape[0]):
        total = total + got[c]
    part[...] = total
    top = folded(jnp.max(jnp.max(total, axis=0), axis=0, keepdims=True), jnp.maximum)
    for n in range(peak.shape[0]):
        peak[n] = top


def fan_kernel(combine, got, out):
    total = got[0]
    for n in range(1, got.shape[0]):
        total = combine(total, got[n])
    for n in range(out.shape[0]):
        out[n] = total


def join_kernel(halves, received, peaks, out):
    chips, planes, rows, width = received.shape
    for c in range(chips):
        for i in range(planes):
            out[c, i] = halves[0, c, i] + received[c, i]
    top = jnp.broadcast_to(jnp.max(peaks[...], axis=0), (rows, 128))
    for c in range(chips):
        for j in range(0, width, 128):
            out[c, planes, :, j : j + 128] = top


def gradient_kernel(got, illum, water, guide, first_depth, gradient, sums):
    planes, rows, width = illum.shape
    top = got[0, planes]
    for c in range(1, got.shape[0]):
        top = jnp.maximum(top, got[c, planes])
    peak = jnp.max(top)
    depth = first_depth[0] + lax.broadcasted_iota(jnp.int32, (rows, width), 0)
    square = jnp.zeros((rows, width), f32)
    along = jnp.zeros((rows, width), f32)
    for i in range(planes):
        image = got[0, i]
        for c in range(1, got.shape[0]):
            image = image + got[c, i]
        value = image / (illum[i] + water_level * peak)
        value = jnp.where(depth >= water[i : i + 1], value, f32(0.0))
        gradient[i] = value
        square += value * value
        along += value * guide[i]
    for k, total in ((0, square), (1, along)):
        line = folded(jnp.sum(total, axis=0, keepdims=True), jnp.add)
        for n in range(sums.shape[0]):
            sums[n, :, k * 128 : (k + 1) * 128] = line


def to_next(cells):
    count = lax.axis_size("brick")
    return lax.ppermute(cells, "brick", [(i, i + 1) for i in range(count - 1)])


def to_previous(cells):
    count = lax.axis_size("brick")
    return lax.ppermute(cells, "brick", [(i + 1, i) for i in range(count - 1)])


def swapped(copies, axis, groups):
    return lax.all_to_all(copies, axis, 0, 0, axis_index_groups=groups, tiled=True)


def fan(combine, got, count):
    return pl.pallas_call(
        functools.partial(fan_kernel, combine),
        out_shape=jax.ShapeDtypeStruct((count,) + got.shape[1:], f32),
        in_specs=vmem(1),
        out_specs=vmem(1)[0],
        compiler_params=params,
        cost_estimate=pl.CostEstimate(flops=10**4, bytes_accessed=10**4, transcendentals=0),
    )(got)


def exchanged(halves):
    parts = lax.axis_size("shot")
    return lax.ppermute(halves[1], "shot", [(i, i ^ 1) for i in range(parts)])


def own_rows(halves):
    return halves[0] + exchanged(halves)


def four_chips(pieces):
    parts = lax.axis_size("shot")
    groups = [[2 * c + core for c in range(parts // 2)] for core in range(2)]
    return lax.all_to_all(pieces, "shot", 0, 0, axis_index_groups=groups, tiled=True)


def per_device(
    adjoint_prev, adjoint_now, forward_snaps, courant, traces, rec_x, rec_y, water_rows, direction
):
    now = adjoint_now
    shots, cells_x, depth_cells, cells_y = now.shape
    parts = lax.axis_size("shot")
    bricks = lax.axis_size("brick")
    rows_part = depth_cells // parts
    columns = 4
    along = [[g + columns * i for i in range(bricks // columns)] for g in range(columns)]
    across = [
        [bricks * s + columns * g + i for s in range(parts) for i in range(columns)]
        for g in range(bricks // columns)
    ]
    beside = [
        [bricks * (2 * c + core) + columns * g + i for core in range(2) for i in range(columns)]
        for c in range(parts // 2)
        for g in range(bricks // columns)
    ]
    shot = lax.axis_index("shot")
    first_row = (lax.axis_index("brick") * cells_x).astype(jnp.int32)[None]
    core = (shot % 2).astype(jnp.int32)[None]
    offset = (shot * rows_part).astype(jnp.int32)
    smem = pl.BlockSpec(memory_space=pltpu.SMEM)
    shape = jax.ShapeDtypeStruct
    halves_shape = shape((2, parts // 2, cells_x, rows_part, cells_y), f32)

    illum_halves = pl.pallas_call(
        illum_kernel,
        out_shape=halves_shape,
        in_specs=vmem(1) + [smem],
        out_specs=vmem(1)[0],
        compiler_params=params,
        cost_estimate=pl.CostEstimate(flops=10**6, bytes_accessed=2 * 10**6, transcendentals=0),
    )(forward_snaps, core)
    illum_mine = own_rows(illum_halves)
    illum_got = four_chips(illum_mine)

    illum_part, own_peak = pl.pallas_call(
        peak_kernel,
        out_shape=(
            shape((cells_x, rows_part, cells_y), f32),
            shape((len(along[0]), 1, 128), f32),
        ),
        in_specs=vmem(1),
        out_specs=tuple(vmem(2)),
        compiler_params=params,
        cost_estimate=pl.CostEstimate(flops=10**5, bytes_accessed=4 * 10**5, transcendentals=0),
    )(illum_got)
    peak = fan(jnp.maximum, swapped(own_peak, "brick", along), len(beside[0]))

    side_shape = shape((2 * shots + 1, 2, depth_cells, cells_y), f32)
    local, head, tail = pl.pallas_call(
        local_kernel,
        out_shape=(shape(now.shape, f32), side_shape, side_shape),
        in_specs=vmem(6) + [smem] + vmem(1),
        out_specs=tuple(vmem(3)),
        scratch_shapes=[pltpu.VMEM((cells_x, cells_y), f32)],
        compiler_params=params,
        cost_estimate=pl.CostEstimate(flops=10**7, bytes_accessed=4 * 10**6, transcendentals=0),
    )(adjoint_prev, now, courant, traces, rec_x, rec_y, first_row, own_peak)
    before = to_next(tail)
    after = to_previous(head)

    image_halves = pl.pallas_call(
        image_kernel,
        out_shape=halves_shape,
        in_specs=vmem(9) + [smem, smem] + vmem(1),
        out_specs=vmem(1)[0],
        scratch_shapes=[
            pltpu.VMEM((shots, cells_x + 4, depth_cells, cells_y), f32),
            pltpu.VMEM((shots, cells_x, cells_y), f32),
        ],
        compiler_params=params,
        cost_estimate=pl.CostEstimate(flops=10**7, bytes_accessed=6 * 10**6, transcendentals=0),
    )(
        local, now, courant, before, after, forward_snaps,
        traces, rec_x, rec_y, first_row, core, peak,
    )
    peaks = swapped(peak, ("shot", "brick"), beside)
    pieces = pl.pallas_call(
        join_kernel,
        out_shape=shape((parts // 2, cells_x + 1, rows_part, cells_y), f32),
        in_specs=vmem(3),
        out_specs=vmem(1)[0],
        compiler_params=params,
        cost_estimate=pl.CostEstimate(flops=10**5, bytes_accessed=10**6, transcendentals=0),
    )(image_halves, exchanged(image_halves), peaks)
    image_got = four_chips(pieces)

    guide = lax.dynamic_slice_in_dim(direction, offset, rows_part, 1)
    gradient, sums = pl.pallas_call(
        gradient_kernel,
        out_shape=(shape((cells_x, rows_part, cells_y), f32), shape((len(along[0]), 1, 256), f32)),
        in_specs=vmem(4) + [smem],
        out_specs=tuple(vmem(2)),
        compiler_params=params,
        cost_estimate=pl.CostEstimate(flops=10**6, bytes_accessed=6 * 10**5, transcendentals=0),
    )(image_got, illum_part, water_rows, guide, offset[None])
    sums = fan(jnp.add, swapped(sums, "brick", along), len(across[0]))
    sums = jnp.sum(swapped(sums, ("shot", "brick"), across), axis=0)
    return (gradient, jnp.sum(sums.reshape(2, 128), axis=1))


def solution(mesh):
    in_specs = (
        P("shot", "brick", None, None),
        P("shot", "brick", None, None),
        P("shot", None, "brick", None, None),
        P("brick", None, None),
        P("shot", None, None),
        P("shot", None),
        P("shot", None),
        P("brick", None),
        P("brick", None, None),
    )
    out_specs = (P("brick", "shot", None), P())
    return jax.shard_map(
        per_device, mesh=mesh, in_specs=in_specs, out_specs=out_specs, check_vma=False
    )
```

```python
import functools

import jax
import jax.numpy as jnp
from jax import lax
from jax.experimental import pallas as pl
from jax.experimental.pallas import tpu as pltpu
from jax.sharding import PartitionSpec as P

far_coef = -1.0 / 12.0
near_coef = 4.0 / 3.0
receiver_depth = 2
water_level = 0.1
f32 = jnp.float32
bf16 = jnp.bfloat16


def vmem(count):
    return [pl.BlockSpec(memory_space=pltpu.VMEM)] * count


mib = 1024 * 1024
params = pltpu.CompilerParams(vmem_limit_bytes=16 * mib)


def band(size, center):
    gap = jnp.abs(
        lax.broadcasted_iota(jnp.int32, (size, size), 0)
        - lax.broadcasted_iota(jnp.int32, (size, size), 1)
    )
    weights = jnp.where(gap == 0, f32(center), f32(0.0))
    weights = jnp.where(gap == 1, f32(16.0), weights)
    return jnp.where(gap == 2, f32(-1.0), weights).astype(bf16)


def split_two(v):
    high = v.astype(bf16)
    return high, (v - high.astype(f32)).astype(bf16)


def in_plane(v, band_z, band_y):
    high, low = split_two(v)
    out = jnp.dot(band_z, high, preferred_element_type=f32)
    out += jnp.dot(band_z, low, preferred_element_type=f32)
    out += jnp.dot(high, band_y, preferred_element_type=f32)
    out += jnp.dot(low, band_y, preferred_element_type=f32)
    return out


def injected(trace, row_x, row_y, first_row, rows, cells_y):
    receivers = trace.shape[1]
    at_x = row_x == first_row + lax.broadcasted_iota(jnp.int32, (rows, receivers), 0)
    at_y = (row_y == lax.broadcasted_iota(jnp.int32, (cells_y, receivers), 0)).astype(f32)
    at_y = at_y.astype(bf16)
    rest = jnp.where(at_x, trace, f32(0.0))
    out = jnp.zeros((rows, cells_y), f32)
    for _ in range(3):
        part = rest.astype(bf16)
        rest = rest - part.astype(f32)
        out += lax.dot_general(
            part, at_y, (((1,), (1,)), ((), ())), preferred_element_type=f32
        )
    return out


def illum_kernel(snaps, core, out):
    shots, steps, planes, depth, width = snaps.shape
    parts = 2 * out.shape[1]
    rows = depth // parts
    mine = core[0]
    for i in range(planes):
        total = None
        for s in range(shots):
            for k in range(steps):
                v = snaps[s, k, i].astype(f32)
                total = v * v if total is None else total + v * v
        for p in range(parts):
            slot = (mine + p % 2) % 2
            out[slot, p // 2, i] = total[p * rows : (p + 1) * rows]


def local_kernel(
    prev, now, courant, traces, rec_x, rec_y, first_row, out, head, tail, plane
):
    shots, planes, depth, width = now.shape
    band_y = band(width, -90.0)
    band_z = band(depth, 0.0)
    for s in range(shots):
        plane[...] = injected(
            traces[s, 0:1], rec_x[s : s + 1], rec_y[s : s + 1], first_row[0], planes, width
        )
        for i in range(planes):
            v = now[s, i]
            total = in_plane(v, band_z, band_y)
            for gap, weight in ((1, 16.0), (2, -1.0)):
                for j in (i - gap, i + gap):
                    if 0 <= j < planes:
                        total += weight * now[s, j]
            out[s, i] = 2.0 * v - prev[s, i] + courant[i] * (total * (1.0 / 12.0))
            out[s, i, receiver_depth : receiver_depth + 1] += plane[i : i + 1]
        for j in range(2):
            head[s, j] = out[s, j]
            tail[s, j] = out[s, planes - 2 + j]
            head[shots + s, j] = now[s, j]
            tail[shots + s, j] = now[s, planes - 2 + j]
    for j in range(2):
        head[2 * shots, j] = courant[j]
        tail[2 * shots, j] = courant[planes - 2 + j]


def image_kernel(
    local, now, courant, before, after, snaps,
    traces, rec_x, rec_y, first_row, core, order, out, first, plane,
):
    shots, planes, depth, width = now.shape
    parts = 2 * out.shape[1]
    rows = depth // parts
    band_y = band(width, -90.0)
    band_z = band(depth, 0.0)
    mine = core[0]
    last = planes - 1
    for s in range(shots):
        first[s, 2] = local[s, 0] + courant[0] * (
            far_coef * before[shots + s, 0] + near_coef * before[shots + s, 1]
        )
        first[s, 3] = local[s, 1] + courant[1] * (far_coef * before[shots + s, 1])
        for i in range(2, planes - 2):
            first[s, i + 2] = local[s, i]
        first[s, planes] = local[s, last - 1] + courant[last - 1] * (far_coef * after[shots + s, 0])
        first[s, planes + 1] = local[s, last] + courant[last] * (
            near_coef * after[shots + s, 0] + far_coef * after[shots + s, 1]
        )
        first[s, 0] = before[s, 0] + before[2 * shots, 0] * (far_coef * now[s, 0])
        first[s, 1] = before[s, 1] + before[2 * shots, 1] * (
            near_coef * now[s, 0] + far_coef * now[s, 1]
        )
        first[s, planes + 2] = after[s, 0] + after[2 * shots, 0] * (
            near_coef * now[s, last] + far_coef * now[s, last - 1]
        )
        first[s, planes + 3] = after[s, 1] + after[2 * shots, 1] * (far_coef * now[s, last])
        plane[s] = injected(
            traces[s, 1:2], rec_x[s : s + 1], rec_y[s : s + 1], first_row[0], planes, width
        )
    at_level = (
        lax.broadcasted_iota(jnp.int32, (depth, width), 0) == receiver_depth
    )
    for i in range(planes):
        image = None
        for s in range(shots):
            v = first[s, i + 2]
            total = in_plane(v, band_z, band_y)
            total += 16.0 * (first[s, i + 1] + first[s, i + 3])
            total -= first[s, i] + first[s, i + 4]
            second = 2.0 * v - now[s, i] + courant[i] * (total * (1.0 / 12.0))
            second += jnp.where(at_level, plane[s, i : i + 1], f32(0.0))
            term = snaps[s, 0, i].astype(f32) * v + snaps[s, 1, i].astype(f32) * second
            image = term if image is None else image + term
        for p in range(parts):
            slot = (mine + p % 2) % 2
            out[slot, p // 2, i] = image[p * rows : (p + 1) * rows]


def folded(line, combine):
    out = line[:, :128]
    for j in range(128, line.shape[1], 128):
        out = combine(out, line[:, j : j + 128])
    return out


def peak_kernel(got, direction, water, first_depth, part, peak, guide, floor):
    span = pl.ds(pl.multiple_of(first_depth[0], guide.shape[1]), guide.shape[1])
    for i in range(guide.shape[0]):
        guide[i] = direction[i, span]
    floor[...] = water[...]
    total = got[0]
    for c in range(1, got.shape[0]):
        total = total + got[c]
    part[...] = total
    top = folded(jnp.max(jnp.max(total, axis=0), axis=0, keepdims=True), jnp.maximum)
    for n in range(peak.shape[0]):
        peak[n] = top


def fan_kernel(combine, got, out):
    total = got[0]
    for n in range(1, got.shape[0]):
        total = combine(total, got[n])
    for n in range(out.shape[0]):
        out[n] = total


def join_kernel(halves, received, peaks, out):
    chips, planes, rows, width = received.shape
    for c in range(chips):
        for i in range(planes):
            out[c, i] = halves[0, c, i] + received[c, i]
    top = jnp.broadcast_to(jnp.max(peaks[...], axis=0), (rows, 128))
    for c in range(chips):
        for j in range(0, width, 128):
            out[c, planes, :, j : j + 128] = top


def gradient_kernel(got, illum, water, guide, first_depth, gradient, sums):
    planes, rows, width = illum.shape
    top = got[0, planes]
    for c in range(1, got.shape[0]):
        top = jnp.maximum(top, got[c, planes])
    peak = jnp.max(top)
    depth = first_depth[0] + lax.broadcasted_iota(jnp.int32, (rows, width), 0)
    square = jnp.zeros((rows, width), f32)
    along = jnp.zeros((rows, width), f32)
    for i in range(planes):
        image = got[0, i]
        for c in range(1, got.shape[0]):
            image = image + got[c, i]
        value = image / (illum[i] + water_level * peak)
        value = jnp.where(depth >= water[i : i + 1], value, f32(0.0))
        gradient[i] = value
        square += value * value
        along += value * guide[i]
    for k, total in ((0, square), (1, along)):
        line = folded(jnp.sum(total, axis=0, keepdims=True), jnp.add)
        for n in range(sums.shape[0]):
            sums[n, :, k * 128 : (k + 1) * 128] = line


def last_kernel(got, value, gradient, sums):
    gradient[...] = value[...]
    total = got[0]
    for n in range(1, got.shape[0]):
        total = total + got[n]
    sums[0] = jnp.sum(total[:, :128])
    sums[1] = jnp.sum(total[:, 128:])


def to_next(cells):
    count = lax.axis_size("brick")
    return lax.ppermute(cells, "brick", [(i, i + 1) for i in range(count - 1)])


def to_previous(cells):
    count = lax.axis_size("brick")
    return lax.ppermute(cells, "brick", [(i + 1, i) for i in range(count - 1)])


def swapped(copies, axis, groups):
    return lax.all_to_all(copies, axis, 0, 0, axis_index_groups=groups, tiled=True)


def fan(combine, got, count):
    return pl.pallas_call(
        functools.partial(fan_kernel, combine),
        out_shape=jax.ShapeDtypeStruct((count,) + got.shape[1:], f32),
        in_specs=vmem(1),
        out_specs=vmem(1)[0],
        compiler_params=params,
        cost_estimate=pl.CostEstimate(flops=10**4, bytes_accessed=10**4, transcendentals=0),
    )(got)


def exchanged(halves):
    parts = lax.axis_size("shot")
    return lax.ppermute(halves[1], "shot", [(i, i ^ 1) for i in range(parts)])


def own_rows(halves):
    return halves[0] + exchanged(halves)


def four_chips(pieces):
    parts = lax.axis_size("shot")
    groups = [[2 * c + core for c in range(parts // 2)] for core in range(2)]
    return lax.all_to_all(pieces, "shot", 0, 0, axis_index_groups=groups, tiled=True)


def per_device(
    adjoint_prev, adjoint_now, forward_snaps, courant, traces, rec_x, rec_y, water_rows, direction
):
    now = adjoint_now
    shots, cells_x, depth_cells, cells_y = now.shape
    parts = lax.axis_size("shot")
    bricks = lax.axis_size("brick")
    rows_part = depth_cells // parts
    columns = 4
    along = [[g + columns * i for i in range(bricks // columns)] for g in range(columns)]
    across = [
        [bricks * s + columns * g + i for s in range(parts) for i in range(columns)]
        for g in range(bricks // columns)
    ]
    beside = [
        [bricks * (2 * c + core) + columns * g + i for core in range(2) for i in range(columns)]
        for c in range(parts // 2)
        for g in range(bricks // columns)
    ]
    shot = lax.axis_index("shot")
    first_row = (lax.axis_index("brick") * cells_x).astype(jnp.int32)[None]
    core = (shot % 2).astype(jnp.int32)[None]
    offset = (shot * rows_part).astype(jnp.int32)
    smem = pl.BlockSpec(memory_space=pltpu.SMEM)
    shape = jax.ShapeDtypeStruct
    halves_shape = shape((2, parts // 2, cells_x, rows_part, cells_y), f32)

    illum_halves = pl.pallas_call(
        illum_kernel,
        out_shape=halves_shape,
        in_specs=vmem(1) + [smem],
        out_specs=vmem(1)[0],
        compiler_params=params,
        cost_estimate=pl.CostEstimate(flops=10**6, bytes_accessed=2 * 10**6, transcendentals=0),
    )(forward_snaps, core)
    illum_mine = own_rows(illum_halves)
    illum_got = four_chips(illum_mine)

    part_shape = shape((cells_x, rows_part, cells_y), f32)
    illum_part, own_peak, guide, floor = pl.pallas_call(
        peak_kernel,
        out_shape=(
            part_shape,
            shape((len(along[0]), 1, 128), f32),
            part_shape,
            shape(water_rows.shape, jnp.int32),
        ),
        in_specs=vmem(3) + [smem],
        out_specs=tuple(vmem(4)),
        compiler_params=params,
        cost_estimate=pl.CostEstimate(flops=10**5, bytes_accessed=4 * 10**5, transcendentals=0),
    )(illum_got, direction, water_rows, offset[None])
    peak = fan(jnp.maximum, swapped(own_peak, "brick", along), len(beside[0]))

    side_shape = shape((2 * shots + 1, 2, depth_cells, cells_y), f32)
    local, head, tail = pl.pallas_call(
        local_kernel,
        out_shape=(shape(now.shape, f32), side_shape, side_shape),
        in_specs=vmem(6) + [smem],
        out_specs=tuple(vmem(3)),
        scratch_shapes=[pltpu.VMEM((cells_x, cells_y), f32)],
        compiler_params=params,
        cost_estimate=pl.CostEstimate(flops=10**7, bytes_accessed=4 * 10**6, transcendentals=0),
    )(adjoint_prev, now, courant, traces, rec_x, rec_y, first_row)
    before = to_next(tail)
    after = to_previous(head)

    image_halves = pl.pallas_call(
        image_kernel,
        out_shape=halves_shape,
        in_specs=vmem(9) + [smem, smem] + vmem(1),
        out_specs=vmem(1)[0],
        scratch_shapes=[
            pltpu.VMEM((shots, cells_x + 4, depth_cells, cells_y), f32),
            pltpu.VMEM((shots, cells_x, cells_y), f32),
        ],
        compiler_params=params,
        cost_estimate=pl.CostEstimate(flops=10**7, bytes_accessed=6 * 10**6, transcendentals=0),
    )(
        local, now, courant, before, after, forward_snaps,
        traces, rec_x, rec_y, first_row, core, peak,
    )
    peaks = swapped(peak, ("shot", "brick"), beside)
    pieces = pl.pallas_call(
        join_kernel,
        out_shape=shape((parts // 2, cells_x + 1, rows_part, cells_y), f32),
        in_specs=vmem(3),
        out_specs=vmem(1)[0],
        compiler_params=params,
        cost_estimate=pl.CostEstimate(flops=10**5, bytes_accessed=10**6, transcendentals=0),
    )(image_halves, exchanged(image_halves), peaks)
    image_got = four_chips(pieces)

    gradient, sums = pl.pallas_call(
        gradient_kernel,
        out_shape=(shape((cells_x, rows_part, cells_y), f32), shape((len(along[0]), 1, 256), f32)),
        in_specs=vmem(4) + [smem],
        out_specs=tuple(vmem(2)),
        compiler_params=params,
        cost_estimate=pl.CostEstimate(flops=10**6, bytes_accessed=6 * 10**5, transcendentals=0),
    )(image_got, illum_part, floor, guide, offset[None])
    sums = fan(jnp.add, swapped(sums, "brick", along), len(across[0]))
    gradient, sums = pl.pallas_call(
        last_kernel,
        out_shape=(shape(gradient.shape, f32), shape((2,), f32)),
        in_specs=vmem(2),
        out_specs=(vmem(1)[0], smem),
        compiler_params=params,
        cost_estimate=pl.CostEstimate(flops=10**4, bytes_accessed=2 * 10**5, transcendentals=0),
    )(swapped(sums, ("shot", "brick"), across), gradient)
    return (gradient, sums)


def solution(mesh):
    in_specs = (
        P("shot", "brick", None, None),
        P("shot", "brick", None, None),
        P("shot", None, "brick", None, None),
        P("brick", None, None),
        P("shot", None, None),
        P("shot", None),
        P("shot", None),
        P("brick", None),
        P("brick", None, None),
    )
    out_specs = (P("brick", "shot", None), P())
    return jax.shard_map(
        per_device, mesh=mesh, in_specs=in_specs, out_specs=out_specs, check_vma=False
    )
```

```python
import functools

import jax
import jax.numpy as jnp
from jax import lax
from jax.experimental import pallas as pl
from jax.experimental.pallas import tpu as pltpu
from jax.sharding import PartitionSpec as P

far_coef = -1.0 / 12.0
near_coef = 4.0 / 3.0
receiver_depth = 2
water_level = 0.1
f32 = jnp.float32
bf16 = jnp.bfloat16


def vmem(count):
    return [pl.BlockSpec(memory_space=pltpu.VMEM)] * count


mib = 1024 * 1024
params = pltpu.CompilerParams(vmem_limit_bytes=16 * mib)


def band(size, center):
    gap = jnp.abs(
        lax.broadcasted_iota(jnp.int32, (size, size), 0)
        - lax.broadcasted_iota(jnp.int32, (size, size), 1)
    )
    weights = jnp.where(gap == 0, f32(center), f32(0.0))
    weights = jnp.where(gap == 1, f32(16.0), weights)
    return jnp.where(gap == 2, f32(-1.0), weights).astype(bf16)


def split_two(v):
    high = v.astype(bf16)
    return high, (v - high.astype(f32)).astype(bf16)


def in_plane(v, band_z, band_y):
    high, low = split_two(v)
    out = jnp.dot(band_z, high, preferred_element_type=f32)
    out += jnp.dot(band_z, low, preferred_element_type=f32)
    out += jnp.dot(high, band_y, preferred_element_type=f32)
    out += jnp.dot(low, band_y, preferred_element_type=f32)
    return out


def injected(trace, row_x, row_y, first_row, rows, cells_y):
    receivers = trace.shape[1]
    at_x = row_x == first_row + lax.broadcasted_iota(jnp.int32, (rows, receivers), 0)
    at_y = (row_y == lax.broadcasted_iota(jnp.int32, (cells_y, receivers), 0)).astype(f32)
    at_y = at_y.astype(bf16)
    rest = jnp.where(at_x, trace, f32(0.0))
    out = jnp.zeros((rows, cells_y), f32)
    for _ in range(3):
        part = rest.astype(bf16)
        rest = rest - part.astype(f32)
        out += lax.dot_general(
            part, at_y, (((1,), (1,)), ((), ())), preferred_element_type=f32
        )
    return out


def illum_kernel(snaps, core, out):
    shots, steps, planes, depth, width = snaps.shape
    parts = 2 * out.shape[1]
    rows = depth // parts
    mine = core[0]
    for i in range(planes):
        total = None
        for s in range(shots):
            for k in range(steps):
                v = snaps[s, k, i].astype(f32)
                total = v * v if total is None else total + v * v
        for p in range(parts):
            slot = (mine + p % 2) % 2
            out[slot, p // 2, i] = total[p * rows : (p + 1) * rows]


def local_kernel(
    prev, now, courant, traces, rec_x, rec_y, first_row, order, out, head, tail, plane
):
    shots, planes, depth, width = now.shape
    band_y = band(width, -90.0)
    band_z = band(depth, 0.0)
    for s in range(shots):
        plane[...] = injected(
            traces[s, 0:1], rec_x[s : s + 1], rec_y[s : s + 1], first_row[0], planes, width
        )
        for i in range(planes):
            v = now[s, i]
            total = in_plane(v, band_z, band_y)
            for gap, weight in ((1, 16.0), (2, -1.0)):
                for j in (i - gap, i + gap):
                    if 0 <= j < planes:
                        total += weight * now[s, j]
            out[s, i] = 2.0 * v - prev[s, i] + courant[i] * (total * (1.0 / 12.0))
            out[s, i, receiver_depth : receiver_depth + 1] += plane[i : i + 1]
        for j in range(2):
            head[s, j] = out[s, j]
            tail[s, j] = out[s, planes - 2 + j]
            head[shots + s, j] = now[s, j]
            tail[shots + s, j] = now[s, planes - 2 + j]
    for j in range(2):
        head[2 * shots, j] = courant[j]
        tail[2 * shots, j] = courant[planes - 2 + j]


def image_kernel(
    local, now, courant, before, after, snaps,
    traces, rec_x, rec_y, first_row, core, order, out, first, plane,
):
    shots, planes, depth, width = now.shape
    parts = 2 * out.shape[1]
    rows = depth // parts
    band_y = band(width, -90.0)
    band_z = band(depth, 0.0)
    mine = core[0]
    last = planes - 1
    for s in range(shots):
        first[s, 2] = local[s, 0] + courant[0] * (
            far_coef * before[shots + s, 0] + near_coef * before[shots + s, 1]
        )
        first[s, 3] = local[s, 1] + courant[1] * (far_coef * before[shots + s, 1])
        for i in range(2, planes - 2):
            first[s, i + 2] = local[s, i]
        first[s, planes] = local[s, last - 1] + courant[last - 1] * (far_coef * after[shots + s, 0])
        first[s, planes + 1] = local[s, last] + courant[last] * (
            near_coef * after[shots + s, 0] + far_coef * after[shots + s, 1]
        )
        first[s, 0] = before[s, 0] + before[2 * shots, 0] * (far_coef * now[s, 0])
        first[s, 1] = before[s, 1] + before[2 * shots, 1] * (
            near_coef * now[s, 0] + far_coef * now[s, 1]
        )
        first[s, planes + 2] = after[s, 0] + after[2 * shots, 0] * (
            near_coef * now[s, last] + far_coef * now[s, last - 1]
        )
        first[s, planes + 3] = after[s, 1] + after[2 * shots, 1] * (far_coef * now[s, last])
        plane[s] = injected(
            traces[s, 1:2], rec_x[s : s + 1], rec_y[s : s + 1], first_row[0], planes, width
        )
    at_level = (
        lax.broadcasted_iota(jnp.int32, (depth, width), 0) == receiver_depth
    )
    for i in range(planes):
        image = None
        for s in range(shots):
            v = first[s, i + 2]
            total = in_plane(v, band_z, band_y)
            total += 16.0 * (first[s, i + 1] + first[s, i + 3])
            total -= first[s, i] + first[s, i + 4]
            second = 2.0 * v - now[s, i] + courant[i] * (total * (1.0 / 12.0))
            second += jnp.where(at_level, plane[s, i : i + 1], f32(0.0))
            term = snaps[s, 0, i].astype(f32) * v + snaps[s, 1, i].astype(f32) * second
            image = term if image is None else image + term
        for p in range(parts):
            slot = (mine + p % 2) % 2
            out[slot, p // 2, i] = image[p * rows : (p + 1) * rows]


def add_kernel(halves, received, traces, rec_x, rec_y, guide, mine, traces_out, x_out, y_out):
    for c in range(mine.shape[0]):
        for i in range(mine.shape[1]):
            mine[c, i] = halves[0, c, i] + received[c, i]
    traces_out[...] = traces[...]
    x_out[...] = rec_x[...]
    y_out[...] = rec_y[...]


def folded(line, combine):
    out = line[:, :128]
    for j in range(128, line.shape[1], 128):
        out = combine(out, line[:, j : j + 128])
    return out


def peak_kernel(got, part, peak):
    total = got[0]
    for c in range(1, got.shape[0]):
        total = total + got[c]
    part[...] = total
    top = folded(jnp.max(jnp.max(total, axis=0), axis=0, keepdims=True), jnp.maximum)
    for n in range(peak.shape[0]):
        peak[n] = top


def fan_kernel(combine, got, out):
    total = got[0]
    for n in range(1, got.shape[0]):
        total = combine(total, got[n])
    for n in range(out.shape[0]):
        out[n] = total


def join_kernel(halves, received, peaks, out):
    chips, planes, rows, width = received.shape
    for c in range(chips):
        for i in range(planes):
            out[c, i] = halves[0, c, i] + received[c, i]
    top = jnp.broadcast_to(jnp.max(peaks[...], axis=0), (rows, 128))
    for c in range(chips):
        for j in range(0, width, 128):
            out[c, planes, :, j : j + 128] = top


def gradient_kernel(got, illum, water, guide, first_depth, gradient, sums):
    planes, rows, width = illum.shape
    top = got[0, planes]
    for c in range(1, got.shape[0]):
        top = jnp.maximum(top, got[c, planes])
    peak = jnp.max(top)
    depth = first_depth[0] + lax.broadcasted_iota(jnp.int32, (rows, width), 0)
    square = jnp.zeros((rows, width), f32)
    along = jnp.zeros((rows, width), f32)
    for i in range(planes):
        image = got[0, i]
        for c in range(1, got.shape[0]):
            image = image + got[c, i]
        value = image / (illum[i] + water_level * peak)
        value = jnp.where(depth >= water[i : i + 1], value, f32(0.0))
        gradient[i] = value
        square += value * value
        along += value * guide[i]
    for k, total in ((0, square), (1, along)):
        line = folded(jnp.sum(total, axis=0, keepdims=True), jnp.add)
        for n in range(sums.shape[0]):
            sums[n, :, k * 128 : (k + 1) * 128] = line


def last_kernel(got, value, gradient, sums):
    gradient[...] = value[...]
    total = got[0]
    for n in range(1, got.shape[0]):
        total = total + got[n]
    sums[0] = jnp.sum(total[:, :128])
    sums[1] = jnp.sum(total[:, 128:])


def to_next(cells):
    count = lax.axis_size("brick")
    return lax.ppermute(cells, "brick", [(i, i + 1) for i in range(count - 1)])


def to_previous(cells):
    count = lax.axis_size("brick")
    return lax.ppermute(cells, "brick", [(i + 1, i) for i in range(count - 1)])


def swapped(copies, axis, groups):
    return lax.all_to_all(copies, axis, 0, 0, axis_index_groups=groups, tiled=True)


def fan(combine, got, count):
    return pl.pallas_call(
        functools.partial(fan_kernel, combine),
        out_shape=jax.ShapeDtypeStruct((count,) + got.shape[1:], f32),
        in_specs=vmem(1),
        out_specs=vmem(1)[0],
        compiler_params=params,
        cost_estimate=pl.CostEstimate(flops=10**4, bytes_accessed=10**4, transcendentals=0),
    )(got)


def exchanged(halves):
    parts = lax.axis_size("shot")
    return lax.ppermute(halves[1], "shot", [(i, i ^ 1) for i in range(parts)])


def four_chips(pieces):
    parts = lax.axis_size("shot")
    groups = [[2 * c + core for c in range(parts // 2)] for core in range(2)]
    return lax.all_to_all(pieces, "shot", 0, 0, axis_index_groups=groups, tiled=True)


def per_device(
    adjoint_prev, adjoint_now, forward_snaps, courant, traces, rec_x, rec_y, water_rows, direction
):
    now = adjoint_now
    shots, cells_x, depth_cells, cells_y = now.shape
    parts = lax.axis_size("shot")
    bricks = lax.axis_size("brick")
    rows_part = depth_cells // parts
    columns = 4
    along = [[g + columns * i for i in range(bricks // columns)] for g in range(columns)]
    across = [
        [bricks * s + columns * g + i for s in range(parts) for i in range(columns)]
        for g in range(bricks // columns)
    ]
    beside = [
        [bricks * (2 * c + core) + columns * g + i for core in range(2) for i in range(columns)]
        for c in range(parts // 2)
        for g in range(bricks // columns)
    ]
    shot = lax.axis_index("shot")
    first_row = (lax.axis_index("brick") * cells_x).astype(jnp.int32)[None]
    core = (shot % 2).astype(jnp.int32)[None]
    offset = (shot * rows_part).astype(jnp.int32)
    smem = pl.BlockSpec(memory_space=pltpu.SMEM)
    shape = jax.ShapeDtypeStruct
    halves_shape = shape((2, parts // 2, cells_x, rows_part, cells_y), f32)

    illum_halves = pl.pallas_call(
        illum_kernel,
        out_shape=halves_shape,
        in_specs=vmem(1) + [smem],
        out_specs=vmem(1)[0],
        compiler_params=params,
        cost_estimate=pl.CostEstimate(flops=10**6, bytes_accessed=2 * 10**6, transcendentals=0),
    )(forward_snaps, core)
    guide = lax.dynamic_slice_in_dim(direction, offset, rows_part, 1)
    illum_mine, traces, rec_x, rec_y = pl.pallas_call(
        add_kernel,
        out_shape=(
            shape(halves_shape.shape[1:], f32),
            shape(traces.shape, f32),
            shape(rec_x.shape, jnp.int32),
            shape(rec_y.shape, jnp.int32),
        ),
        in_specs=vmem(6),
        out_specs=tuple(vmem(4)),
        compiler_params=params,
        cost_estimate=pl.CostEstimate(flops=10**5, bytes_accessed=10**6, transcendentals=0),
    )(illum_halves, exchanged(illum_halves), traces, rec_x, rec_y, guide)
    illum_got = four_chips(illum_mine)

    illum_part, own_peak = pl.pallas_call(
        peak_kernel,
        out_shape=(
            shape((cells_x, rows_part, cells_y), f32),
            shape((len(along[0]), 1, 128), f32),
        ),
        in_specs=vmem(1),
        out_specs=tuple(vmem(2)),
        compiler_params=params,
        cost_estimate=pl.CostEstimate(flops=10**5, bytes_accessed=4 * 10**5, transcendentals=0),
    )(illum_got)
    peak = fan(jnp.maximum, swapped(own_peak, "brick", along), len(beside[0]))

    side_shape = shape((2 * shots + 1, 2, depth_cells, cells_y), f32)
    local, head, tail = pl.pallas_call(
        local_kernel,
        out_shape=(shape(now.shape, f32), side_shape, side_shape),
        in_specs=vmem(6) + [smem] + vmem(1),
        out_specs=tuple(vmem(3)),
        scratch_shapes=[pltpu.VMEM((cells_x, cells_y), f32)],
        compiler_params=params,
        cost_estimate=pl.CostEstimate(flops=10**7, bytes_accessed=4 * 10**6, transcendentals=0),
    )(adjoint_prev, now, courant, traces, rec_x, rec_y, first_row, own_peak)
    before = to_next(tail)
    after = to_previous(head)

    image_halves = pl.pallas_call(
        image_kernel,
        out_shape=halves_shape,
        in_specs=vmem(9) + [smem, smem] + vmem(1),
        out_specs=vmem(1)[0],
        scratch_shapes=[
            pltpu.VMEM((shots, cells_x + 4, depth_cells, cells_y), f32),
            pltpu.VMEM((shots, cells_x, cells_y), f32),
        ],
        compiler_params=params,
        cost_estimate=pl.CostEstimate(flops=10**7, bytes_accessed=6 * 10**6, transcendentals=0),
    )(
        local, now, courant, before, after, forward_snaps,
        traces, rec_x, rec_y, first_row, core, peak,
    )
    peaks = swapped(peak, ("shot", "brick"), beside)
    pieces = pl.pallas_call(
        join_kernel,
        out_shape=shape((parts // 2, cells_x + 1, rows_part, cells_y), f32),
        in_specs=vmem(3),
        out_specs=vmem(1)[0],
        compiler_params=params,
        cost_estimate=pl.CostEstimate(flops=10**5, bytes_accessed=10**6, transcendentals=0),
    )(image_halves, exchanged(image_halves), peaks)
    image_got = four_chips(pieces)

    gradient, sums = pl.pallas_call(
        gradient_kernel,
        out_shape=(shape((cells_x, rows_part, cells_y), f32), shape((len(along[0]), 1, 256), f32)),
        in_specs=vmem(4) + [smem],
        out_specs=tuple(vmem(2)),
        compiler_params=params,
        cost_estimate=pl.CostEstimate(flops=10**6, bytes_accessed=6 * 10**5, transcendentals=0),
    )(image_got, illum_part, water_rows, guide, offset[None])
    sums = fan(jnp.add, swapped(sums, "brick", along), len(across[0]))
    gradient, sums = pl.pallas_call(
        last_kernel,
        out_shape=(shape(gradient.shape, f32), shape((2,), f32)),
        in_specs=vmem(2),
        out_specs=(vmem(1)[0], smem),
        compiler_params=params,
        cost_estimate=pl.CostEstimate(flops=10**4, bytes_accessed=2 * 10**5, transcendentals=0),
    )(swapped(sums, ("shot", "brick"), across), gradient)
    return (gradient, sums)


def solution(mesh):
    in_specs = (
        P("shot", "brick", None, None),
        P("shot", "brick", None, None),
        P("shot", None, "brick", None, None),
        P("brick", None, None),
        P("shot", None, None),
        P("shot", None),
        P("shot", None),
        P("brick", None),
        P("brick", None, None),
    )
    out_specs = (P("brick", "shot", None), P())
    return jax.shard_map(
        per_device, mesh=mesh, in_specs=in_specs, out_specs=out_specs, check_vma=False
    )
```

```python
import functools

import jax
import jax.numpy as jnp
from jax import lax
from jax.experimental import pallas as pl
from jax.experimental.pallas import tpu as pltpu
from jax.sharding import PartitionSpec as P

far_coef = -1.0 / 12.0
near_coef = 4.0 / 3.0
receiver_depth = 2
water_level = 0.1
f32 = jnp.float32
bf16 = jnp.bfloat16


def vmem(count):
    return [pl.BlockSpec(memory_space=pltpu.VMEM)] * count


mib = 1024 * 1024
params = pltpu.CompilerParams(vmem_limit_bytes=16 * mib)


def band(size, center):
    gap = jnp.abs(
        lax.broadcasted_iota(jnp.int32, (size, size), 0)
        - lax.broadcasted_iota(jnp.int32, (size, size), 1)
    )
    weights = jnp.where(gap == 0, f32(center), f32(0.0))
    weights = jnp.where(gap == 1, f32(16.0), weights)
    return jnp.where(gap == 2, f32(-1.0), weights).astype(bf16)


def split_two(v):
    high = v.astype(bf16)
    return high, (v - high.astype(f32)).astype(bf16)


def in_plane(v, band_z, band_y):
    high, low = split_two(v)
    out = jnp.dot(band_z, high, preferred_element_type=f32)
    out += jnp.dot(band_z, low, preferred_element_type=f32)
    out += jnp.dot(high, band_y, preferred_element_type=f32)
    out += jnp.dot(low, band_y, preferred_element_type=f32)
    return out


def injected(trace, row_x, row_y, first_row, rows, cells_y):
    receivers = trace.shape[1]
    at_x = row_x == first_row + lax.broadcasted_iota(jnp.int32, (rows, receivers), 0)
    at_y = (row_y == lax.broadcasted_iota(jnp.int32, (cells_y, receivers), 0)).astype(f32)
    at_y = at_y.astype(bf16)
    rest = jnp.where(at_x, trace, f32(0.0))
    out = jnp.zeros((rows, cells_y), f32)
    for _ in range(3):
        part = rest.astype(bf16)
        rest = rest - part.astype(f32)
        out += lax.dot_general(
            part, at_y, (((1,), (1,)), ((), ())), preferred_element_type=f32
        )
    return out


def illum_kernel(snaps, core, first_row, first_depth, out):
    shots, steps, planes, depth, width = snaps.shape
    parts = 2 * out.shape[1]
    rows = depth // parts
    mine = core[0]
    for i in range(planes):
        total = None
        for s in range(shots):
            for k in range(steps):
                v = snaps[s, k, i].astype(f32)
                total = v * v if total is None else total + v * v
        for p in range(parts):
            slot = (mine + p % 2) % 2
            out[slot, p // 2, i] = total[p * rows : (p + 1) * rows]


def local_kernel(prev, now, courant, out, head, tail):
    shots, planes, depth, width = now.shape
    band_y = band(width, -90.0)
    band_z = band(depth, 0.0)
    for s in range(shots):
        for i in range(planes):
            v = now[s, i]
            total = in_plane(v, band_z, band_y)
            for gap, weight in ((1, 16.0), (2, -1.0)):
                for j in (i - gap, i + gap):
                    if 0 <= j < planes:
                        total += weight * now[s, j]
            out[s, i] = 2.0 * v - prev[s, i] + courant[i] * (total * (1.0 / 12.0))
        for j in range(2):
            head[s, j] = out[s, j]
            tail[s, j] = out[s, planes - 2 + j]
            head[shots + s, j] = now[s, j]
            tail[shots + s, j] = now[s, planes - 2 + j]
    for j in range(2):
        head[2 * shots, j] = courant[j]
        tail[2 * shots, j] = courant[planes - 2 + j]


def image_kernel(
    local, now, courant, before, after, snaps, traces, rec_x, rec_y, first_row, core, order,
    out, first, injections,
):
    shots, planes, depth, width = now.shape
    parts = 2 * out.shape[1]
    rows = depth // parts
    band_y = band(width, -90.0)
    band_z = band(depth, 0.0)
    mine = core[0]
    last = planes - 1
    for s in range(shots):
        for k in range(2):
            injections[s, k] = injected(
                traces[s, k : k + 1], rec_x[s : s + 1], rec_y[s : s + 1],
                first_row[0] - 2, injections.shape[2], width,
            )
        first[s, 2] = local[s, 0] + courant[0] * (
            far_coef * before[shots + s, 0] + near_coef * before[shots + s, 1]
        )
        first[s, 3] = local[s, 1] + courant[1] * (far_coef * before[shots + s, 1])
        for i in range(2, planes - 2):
            first[s, i + 2] = local[s, i]
        first[s, planes] = local[s, last - 1] + courant[last - 1] * (far_coef * after[shots + s, 0])
        first[s, planes + 1] = local[s, last] + courant[last] * (
            near_coef * after[shots + s, 0] + far_coef * after[shots + s, 1]
        )
        first[s, 0] = before[s, 0] + before[2 * shots, 0] * (far_coef * now[s, 0])
        first[s, 1] = before[s, 1] + before[2 * shots, 1] * (
            near_coef * now[s, 0] + far_coef * now[s, 1]
        )
        first[s, planes + 2] = after[s, 0] + after[2 * shots, 0] * (
            near_coef * now[s, last] + far_coef * now[s, last - 1]
        )
        first[s, planes + 3] = after[s, 1] + after[2 * shots, 1] * (far_coef * now[s, last])
        for i in range(planes + 4):
            first[s, i, receiver_depth : receiver_depth + 1] += injections[s, 0, i : i + 1]
    at_level = (
        lax.broadcasted_iota(jnp.int32, (depth, width), 0) == receiver_depth
    )
    for i in range(planes):
        image = None
        for s in range(shots):
            v = first[s, i + 2]
            total = in_plane(v, band_z, band_y)
            total += 16.0 * (first[s, i + 1] + first[s, i + 3])
            total -= first[s, i] + first[s, i + 4]
            second = 2.0 * v - now[s, i] + courant[i] * (total * (1.0 / 12.0))
            second += jnp.where(at_level, injections[s, 1, i + 2 : i + 3], f32(0.0))
            term = snaps[s, 0, i].astype(f32) * v + snaps[s, 1, i].astype(f32) * second
            image = term if image is None else image + term
        for p in range(parts):
            slot = (mine + p % 2) % 2
            out[slot, p // 2, i] = image[p * rows : (p + 1) * rows]


def folded(line, combine):
    out = line[:, :128]
    for j in range(128, line.shape[1], 128):
        out = combine(out, line[:, j : j + 128])
    return out


def peak_kernel(got, part, peak):
    total = got[0]
    for c in range(1, got.shape[0]):
        total = total + got[c]
    part[...] = total
    top = folded(jnp.max(jnp.max(total, axis=0), axis=0, keepdims=True), jnp.maximum)
    for n in range(peak.shape[0]):
        peak[n] = top


def fan_kernel(combine, got, out):
    total = got[0]
    for n in range(1, got.shape[0]):
        total = combine(total, got[n])
    for n in range(out.shape[0]):
        out[n] = total


def join_kernel(halves, received, peaks, out):
    chips, planes, rows, width = received.shape
    for c in range(chips):
        for i in range(planes):
            out[c, i] = halves[0, c, i] + received[c, i]
    top = jnp.broadcast_to(jnp.max(peaks[...], axis=0), (rows, 128))
    for c in range(chips):
        for j in range(0, width, 128):
            out[c, planes, :, j : j + 128] = top


def gradient_kernel(got, illum, water, direction, first_depth, gradient, sums):
    planes, rows, width = illum.shape
    top = got[0, planes]
    for c in range(1, got.shape[0]):
        top = jnp.maximum(top, got[c, planes])
    peak = jnp.max(top)
    span = pl.ds(pl.multiple_of(first_depth[0], rows), rows)
    depth = first_depth[0] + lax.broadcasted_iota(jnp.int32, (rows, width), 0)
    square = jnp.zeros((rows, width), f32)
    along = jnp.zeros((rows, width), f32)
    for i in range(planes):
        image = got[0, i]
        for c in range(1, got.shape[0]):
            image = image + got[c, i]
        value = image / (illum[i] + water_level * peak)
        value = jnp.where(depth >= water[i : i + 1], value, f32(0.0))
        gradient[i] = value
        square += value * value
        along += value * direction[i, span]
    for k, total in ((0, square), (1, along)):
        line = folded(jnp.sum(total, axis=0, keepdims=True), jnp.add)
        for n in range(sums.shape[0]):
            sums[n, :, k * 128 : (k + 1) * 128] = line


def last_kernel(got, value, gradient, sums):
    gradient[...] = value[...]
    total = got[0]
    for n in range(1, got.shape[0]):
        total = total + got[n]
    sums[0] = jnp.sum(total[:, :128])
    sums[1] = jnp.sum(total[:, 128:])


def to_next(cells):
    count = lax.axis_size("brick")
    return lax.ppermute(cells, "brick", [(i, i + 1) for i in range(count - 1)])


def to_previous(cells):
    count = lax.axis_size("brick")
    return lax.ppermute(cells, "brick", [(i + 1, i) for i in range(count - 1)])


def swapped(copies, axis, groups):
    return lax.all_to_all(copies, axis, 0, 0, axis_index_groups=groups, tiled=True)


def fan(combine, got, count):
    return pl.pallas_call(
        functools.partial(fan_kernel, combine),
        out_shape=jax.ShapeDtypeStruct((count,) + got.shape[1:], f32),
        in_specs=vmem(1),
        out_specs=vmem(1)[0],
        compiler_params=params,
        cost_estimate=pl.CostEstimate(flops=10**4, bytes_accessed=10**4, transcendentals=0),
    )(got)


def exchanged(halves):
    parts = lax.axis_size("shot")
    return lax.ppermute(halves[1], "shot", [(i, i ^ 1) for i in range(parts)])


def four_chips(pieces):
    parts = lax.axis_size("shot")
    groups = [[2 * c + core for c in range(parts // 2)] for core in range(2)]
    return lax.all_to_all(pieces, "shot", 0, 0, axis_index_groups=groups, tiled=True)


def per_device(
    adjoint_prev, adjoint_now, forward_snaps, courant, traces, rec_x, rec_y, water_rows, direction
):
    now = adjoint_now
    shots, cells_x, depth_cells, cells_y = now.shape
    parts = lax.axis_size("shot")
    bricks = lax.axis_size("brick")
    rows_part = depth_cells // parts
    columns = 4
    along = [[g + columns * i for i in range(bricks // columns)] for g in range(columns)]
    across = [
        [bricks * s + columns * g + i for s in range(parts) for i in range(columns)]
        for g in range(bricks // columns)
    ]
    beside = [
        [bricks * (2 * c + core) + columns * g + i for core in range(2) for i in range(columns)]
        for c in range(parts // 2)
        for g in range(bricks // columns)
    ]
    shot = lax.axis_index("shot")
    first_row = (lax.axis_index("brick") * cells_x).astype(jnp.int32)[None]
    core = (shot % 2).astype(jnp.int32)[None]
    offset = (shot * rows_part).astype(jnp.int32)
    smem = pl.BlockSpec(memory_space=pltpu.SMEM)
    shape = jax.ShapeDtypeStruct
    halves_shape = shape((2, parts // 2, cells_x, rows_part, cells_y), f32)

    illum_halves = pl.pallas_call(
        illum_kernel,
        out_shape=halves_shape,
        in_specs=vmem(1) + [smem, smem, smem],
        out_specs=vmem(1)[0],
        compiler_params=params,
        cost_estimate=pl.CostEstimate(flops=10**6, bytes_accessed=2 * 10**6, transcendentals=0),
    )(forward_snaps, core, first_row, offset[None])
    illum_mine = illum_halves[0] + exchanged(illum_halves)
    illum_got = four_chips(illum_mine)

    illum_part, own_peak = pl.pallas_call(
        peak_kernel,
        out_shape=(
            shape((cells_x, rows_part, cells_y), f32),
            shape((len(along[0]), 1, 128), f32),
        ),
        in_specs=vmem(1),
        out_specs=tuple(vmem(2)),
        compiler_params=params,
        cost_estimate=pl.CostEstimate(flops=10**5, bytes_accessed=4 * 10**5, transcendentals=0),
    )(illum_got)
    peak = fan(jnp.maximum, swapped(own_peak, "brick", along), len(beside[0]))

    side_shape = shape((2 * shots + 1, 2, depth_cells, cells_y), f32)
    local, head, tail = pl.pallas_call(
        local_kernel,
        out_shape=(shape(now.shape, f32), side_shape, side_shape),
        in_specs=vmem(3),
        out_specs=tuple(vmem(3)),
        compiler_params=params,
        cost_estimate=pl.CostEstimate(flops=10**7, bytes_accessed=4 * 10**6, transcendentals=0),
    )(adjoint_prev, now, courant)
    before = to_next(tail)
    after = to_previous(head)

    image_halves = pl.pallas_call(
        image_kernel,
        out_shape=halves_shape,
        in_specs=vmem(9) + [smem, smem] + vmem(1),
        out_specs=vmem(1)[0],
        scratch_shapes=[
            pltpu.VMEM((shots, cells_x + 4, depth_cells, cells_y), f32),
            pltpu.VMEM((shots, 2, cells_x + 8, cells_y), f32),
        ],
        compiler_params=params,
        cost_estimate=pl.CostEstimate(flops=10**7, bytes_accessed=6 * 10**6, transcendentals=0),
    )(
        local, now, courant, before, after, forward_snaps,
        traces, rec_x, rec_y, first_row, core, peak,
    )
    peaks = swapped(peak, ("shot", "brick"), beside)
    pieces = pl.pallas_call(
        join_kernel,
        out_shape=shape((parts // 2, cells_x + 1, rows_part, cells_y), f32),
        in_specs=vmem(3),
        out_specs=vmem(1)[0],
        compiler_params=params,
        cost_estimate=pl.CostEstimate(flops=10**5, bytes_accessed=10**6, transcendentals=0),
    )(image_halves, exchanged(image_halves), peaks)
    image_got = four_chips(pieces)

    gradient, sums = pl.pallas_call(
        gradient_kernel,
        out_shape=(shape((cells_x, rows_part, cells_y), f32), shape((len(along[0]), 1, 256), f32)),
        in_specs=vmem(4) + [smem],
        out_specs=tuple(vmem(2)),
        compiler_params=params,
        cost_estimate=pl.CostEstimate(flops=10**6, bytes_accessed=6 * 10**5, transcendentals=0),
    )(image_got, illum_part, water_rows, direction, offset[None])
    sums = fan(jnp.add, swapped(sums, "brick", along), len(across[0]))
    gradient, sums = pl.pallas_call(
        last_kernel,
        out_shape=(shape(gradient.shape, f32), shape((2,), f32)),
        in_specs=vmem(2),
        out_specs=(vmem(1)[0], smem),
        compiler_params=params,
        cost_estimate=pl.CostEstimate(flops=10**4, bytes_accessed=2 * 10**5, transcendentals=0),
    )(swapped(sums, ("shot", "brick"), across), gradient)
    return (gradient, sums)


def solution(mesh):
    in_specs = (
        P("shot", "brick", None, None),
        P("shot", "brick", None, None),
        P("shot", None, "brick", None, None),
        P("brick", None, None),
        P("shot", None, None),
        P("shot", None),
        P("shot", None),
        P("brick", None),
        P("brick", None, None),
    )
    out_specs = (P("brick", "shot", None), P())
    return jax.shard_map(
        per_device, mesh=mesh, in_specs=in_specs, out_specs=out_specs, check_vma=False
    )
```

```python
import functools

import jax
import jax.numpy as jnp
from jax import lax
from jax.experimental import pallas as pl
from jax.experimental.pallas import tpu as pltpu
from jax.sharding import PartitionSpec as P

far_coef = -1.0 / 12.0
near_coef = 4.0 / 3.0
receiver_depth = 2
water_level = 0.1
f32 = jnp.float32
bf16 = jnp.bfloat16


def vmem(count):
    return [pl.BlockSpec(memory_space=pltpu.VMEM)] * count


mib = 1024 * 1024
params = pltpu.CompilerParams(vmem_limit_bytes=16 * mib)


def band(size, center):
    gap = jnp.abs(
        lax.broadcasted_iota(jnp.int32, (size, size), 0)
        - lax.broadcasted_iota(jnp.int32, (size, size), 1)
    )
    weights = jnp.where(gap == 0, f32(center), f32(0.0))
    weights = jnp.where(gap == 1, f32(16.0), weights)
    return jnp.where(gap == 2, f32(-1.0), weights).astype(bf16)


def split_two(v):
    high = v.astype(bf16)
    return high, (v - high.astype(f32)).astype(bf16)


def in_plane(v, band_z, band_y):
    high, low = split_two(v)
    out = jnp.dot(band_z, high, preferred_element_type=f32)
    out += jnp.dot(band_z, low, preferred_element_type=f32)
    out += jnp.dot(high, band_y, preferred_element_type=f32)
    out += jnp.dot(low, band_y, preferred_element_type=f32)
    return out


def injected(trace, row_x, row_y, first_row, rows, cells_y):
    receivers = trace.shape[1]
    at_x = row_x == first_row + lax.broadcasted_iota(jnp.int32, (rows, receivers), 0)
    at_y = (row_y == lax.broadcasted_iota(jnp.int32, (cells_y, receivers), 0)).astype(f32)
    at_y = at_y.astype(bf16)
    rest = jnp.where(at_x, trace, f32(0.0))
    out = jnp.zeros((rows, cells_y), f32)
    for _ in range(3):
        part = rest.astype(bf16)
        rest = rest - part.astype(f32)
        out += lax.dot_general(
            part, at_y, (((1,), (1,)), ((), ())), preferred_element_type=f32
        )
    return out


def illum_kernel(snaps, core, first_row, first_depth, out):
    shots, steps, planes, depth, width = snaps.shape
    parts = 2 * out.shape[1]
    rows = depth // parts
    mine = core[0]
    for i in range(planes):
        total = None
        for s in range(shots):
            for k in range(steps):
                v = snaps[s, k, i].astype(f32)
                total = v * v if total is None else total + v * v
        for p in range(parts):
            slot = (mine + p % 2) % 2
            out[slot, p // 2, i] = total[p * rows : (p + 1) * rows]


def local_kernel(now, courant, out):
    shots, planes, depth, width = now.shape
    band_y = band(width, -90.0)
    band_z = band(depth, 0.0)
    for s in range(shots):
        for i in range(planes):
            v = now[s, i]
            total = in_plane(v, band_z, band_y)
            for gap, weight in ((1, 16.0), (2, -1.0)):
                for j in (i - gap, i + gap):
                    if 0 <= j < planes:
                        total += weight * now[s, j]
            out[s, i] = 2.0 * v + courant[i] * (total * (1.0 / 12.0))


def edges_kernel(
    local, prev, now, courant, traces, rec_x, rec_y, head, tail, traces_out, x_out, y_out
):
    traces_out[...] = traces[...]
    x_out[...] = rec_x[...]
    y_out[...] = rec_y[...]
    shots, planes, depth, width = now.shape
    for side, start in ((head, 0), (tail, planes - 2)):
        for j in range(2):
            for s in range(shots):
                side[s, j] = local[s, start + j] - prev[s, start + j]
                side[shots + s, j] = now[s, start + j]
            side[2 * shots, j] = courant[start + j]


def image_kernel(
    local, prev, now, courant, before, after, snaps, traces, rec_x, rec_y, first_row, core, order,
    out, first, injections,
):
    shots, planes, depth, width = now.shape
    parts = 2 * out.shape[1]
    rows = depth // parts
    band_y = band(width, -90.0)
    band_z = band(depth, 0.0)
    mine = core[0]
    last = planes - 1
    for s in range(shots):
        for k in range(2):
            injections[s, k] = injected(
                traces[s, k : k + 1], rec_x[s : s + 1], rec_y[s : s + 1],
                first_row[0] - 2, injections.shape[2], width,
            )
        first[s, 2] = local[s, 0] - prev[s, 0] + courant[0] * (
            far_coef * before[shots + s, 0] + near_coef * before[shots + s, 1]
        )
        first[s, 3] = local[s, 1] - prev[s, 1] + courant[1] * (far_coef * before[shots + s, 1])
        for i in range(2, planes - 2):
            first[s, i + 2] = local[s, i] - prev[s, i]
        first[s, planes] = local[s, last - 1] - prev[s, last - 1] + courant[last - 1] * (
            far_coef * after[shots + s, 0]
        )
        first[s, planes + 1] = local[s, last] - prev[s, last] + courant[last] * (
            near_coef * after[shots + s, 0] + far_coef * after[shots + s, 1]
        )
        first[s, 0] = before[s, 0] + before[2 * shots, 0] * (far_coef * now[s, 0])
        first[s, 1] = before[s, 1] + before[2 * shots, 1] * (
            near_coef * now[s, 0] + far_coef * now[s, 1]
        )
        first[s, planes + 2] = after[s, 0] + after[2 * shots, 0] * (
            near_coef * now[s, last] + far_coef * now[s, last - 1]
        )
        first[s, planes + 3] = after[s, 1] + after[2 * shots, 1] * (far_coef * now[s, last])
        for i in range(planes + 4):
            first[s, i, receiver_depth : receiver_depth + 1] += injections[s, 0, i : i + 1]
    at_level = (
        lax.broadcasted_iota(jnp.int32, (depth, width), 0) == receiver_depth
    )
    for i in range(planes):
        image = None
        for s in range(shots):
            v = first[s, i + 2]
            total = in_plane(v, band_z, band_y)
            total += 16.0 * (first[s, i + 1] + first[s, i + 3])
            total -= first[s, i] + first[s, i + 4]
            second = 2.0 * v - now[s, i] + courant[i] * (total * (1.0 / 12.0))
            second += jnp.where(at_level, injections[s, 1, i + 2 : i + 3], f32(0.0))
            term = snaps[s, 0, i].astype(f32) * v + snaps[s, 1, i].astype(f32) * second
            image = term if image is None else image + term
        for p in range(parts):
            slot = (mine + p % 2) % 2
            out[slot, p // 2, i] = image[p * rows : (p + 1) * rows]


def folded(line, combine):
    out = line[:, :128]
    for j in range(128, line.shape[1], 128):
        out = combine(out, line[:, j : j + 128])
    return out


def peak_kernel(got, part, peak):
    total = got[0]
    for c in range(1, got.shape[0]):
        total = total + got[c]
    part[...] = total
    top = folded(jnp.max(jnp.max(total, axis=0), axis=0, keepdims=True), jnp.maximum)
    for n in range(peak.shape[0]):
        peak[n] = top


def fan_kernel(combine, got, out):
    total = got[0]
    for n in range(1, got.shape[0]):
        total = combine(total, got[n])
    for n in range(out.shape[0]):
        out[n] = total


def join_kernel(halves, received, peaks, out):
    chips, planes, rows, width = received.shape
    for c in range(chips):
        for i in range(planes):
            out[c, i] = halves[0, c, i] + received[c, i]
    top = jnp.broadcast_to(jnp.max(peaks[...], axis=0), (rows, 128))
    for c in range(chips):
        for j in range(0, width, 128):
            out[c, planes, :, j : j + 128] = top


def gradient_kernel(got, illum, water, direction, first_depth, gradient, sums):
    planes, rows, width = illum.shape
    top = got[0, planes]
    for c in range(1, got.shape[0]):
        top = jnp.maximum(top, got[c, planes])
    peak = jnp.max(top)
    span = pl.ds(pl.multiple_of(first_depth[0], rows), rows)
    depth = first_depth[0] + lax.broadcasted_iota(jnp.int32, (rows, width), 0)
    square = jnp.zeros((rows, width), f32)
    along = jnp.zeros((rows, width), f32)
    for i in range(planes):
        image = got[0, i]
        for c in range(1, got.shape[0]):
            image = image + got[c, i]
        value = image / (illum[i] + water_level * peak)
        value = jnp.where(depth >= water[i : i + 1], value, f32(0.0))
        gradient[i] = value
        square += value * value
        along += value * direction[i, span]
    for k, total in ((0, square), (1, along)):
        line = folded(jnp.sum(total, axis=0, keepdims=True), jnp.add)
        for n in range(sums.shape[0]):
            sums[n, :, k * 128 : (k + 1) * 128] = line


def last_kernel(got, value, gradient, sums):
    gradient[...] = value[...]
    total = got[0]
    for n in range(1, got.shape[0]):
        total = total + got[n]
    sums[0] = jnp.sum(total[:, :128])
    sums[1] = jnp.sum(total[:, 128:])


def to_next(cells):
    count = lax.axis_size("brick")
    return lax.ppermute(cells, "brick", [(i, i + 1) for i in range(count - 1)])


def to_previous(cells):
    count = lax.axis_size("brick")
    return lax.ppermute(cells, "brick", [(i + 1, i) for i in range(count - 1)])


def swapped(copies, axis, groups):
    return lax.all_to_all(copies, axis, 0, 0, axis_index_groups=groups, tiled=True)


def fan(combine, got, count):
    return pl.pallas_call(
        functools.partial(fan_kernel, combine),
        out_shape=jax.ShapeDtypeStruct((count,) + got.shape[1:], f32),
        in_specs=vmem(1),
        out_specs=vmem(1)[0],
        compiler_params=params,
        cost_estimate=pl.CostEstimate(flops=10**4, bytes_accessed=10**4, transcendentals=0),
    )(got)


def exchanged(halves):
    parts = lax.axis_size("shot")
    return lax.ppermute(halves[1], "shot", [(i, i ^ 1) for i in range(parts)])


def four_chips(pieces):
    parts = lax.axis_size("shot")
    groups = [[2 * c + core for c in range(parts // 2)] for core in range(2)]
    return lax.all_to_all(pieces, "shot", 0, 0, axis_index_groups=groups, tiled=True)


def per_device(
    adjoint_prev, adjoint_now, forward_snaps, courant, traces, rec_x, rec_y, water_rows, direction
):
    now = adjoint_now
    shots, cells_x, depth_cells, cells_y = now.shape
    parts = lax.axis_size("shot")
    bricks = lax.axis_size("brick")
    rows_part = depth_cells // parts
    columns = 4
    along = [[g + columns * i for i in range(bricks // columns)] for g in range(columns)]
    across = [
        [bricks * s + columns * g + i for s in range(parts) for i in range(columns)]
        for g in range(bricks // columns)
    ]
    beside = [
        [bricks * (2 * c + core) + columns * g + i for core in range(2) for i in range(columns)]
        for c in range(parts // 2)
        for g in range(bricks // columns)
    ]
    shot = lax.axis_index("shot")
    first_row = (lax.axis_index("brick") * cells_x).astype(jnp.int32)[None]
    core = (shot % 2).astype(jnp.int32)[None]
    offset = (shot * rows_part).astype(jnp.int32)
    smem = pl.BlockSpec(memory_space=pltpu.SMEM)
    shape = jax.ShapeDtypeStruct
    halves_shape = shape((2, parts // 2, cells_x, rows_part, cells_y), f32)

    illum_halves = pl.pallas_call(
        illum_kernel,
        out_shape=halves_shape,
        in_specs=vmem(1) + [smem, smem, smem],
        out_specs=vmem(1)[0],
        compiler_params=params,
        cost_estimate=pl.CostEstimate(flops=10**6, bytes_accessed=2 * 10**6, transcendentals=0),
    )(forward_snaps, core, first_row, offset[None])
    illum_mine = illum_halves[0] + exchanged(illum_halves)
    illum_got = four_chips(illum_mine)

    illum_part, own_peak = pl.pallas_call(
        peak_kernel,
        out_shape=(
            shape((cells_x, rows_part, cells_y), f32),
            shape((len(along[0]), 1, 128), f32),
        ),
        in_specs=vmem(1),
        out_specs=tuple(vmem(2)),
        compiler_params=params,
        cost_estimate=pl.CostEstimate(flops=10**5, bytes_accessed=4 * 10**5, transcendentals=0),
    )(illum_got)
    peak = fan(jnp.maximum, swapped(own_peak, "brick", along), len(beside[0]))

    side_shape = shape((2 * shots + 1, 2, depth_cells, cells_y), f32)
    local = pl.pallas_call(
        local_kernel,
        out_shape=shape(now.shape, f32),
        in_specs=vmem(2),
        out_specs=vmem(1)[0],
        compiler_params=params,
        cost_estimate=pl.CostEstimate(flops=10**7, bytes_accessed=4 * 10**6, transcendentals=0),
    )(now, courant)
    head, tail, traces, rec_x, rec_y = pl.pallas_call(
        edges_kernel,
        out_shape=(
            side_shape,
            side_shape,
            shape(traces.shape, f32),
            shape(rec_x.shape, jnp.int32),
            shape(rec_y.shape, jnp.int32),
        ),
        in_specs=vmem(7),
        out_specs=tuple(vmem(5)),
        compiler_params=params,
        cost_estimate=pl.CostEstimate(flops=10**5, bytes_accessed=10**6, transcendentals=0),
    )(local, adjoint_prev, now, courant, traces, rec_x, rec_y)
    before = to_next(tail)
    after = to_previous(head)

    image_halves = pl.pallas_call(
        image_kernel,
        out_shape=halves_shape,
        in_specs=vmem(10) + [smem, smem] + vmem(1),
        out_specs=vmem(1)[0],
        scratch_shapes=[
            pltpu.VMEM((shots, cells_x + 4, depth_cells, cells_y), f32),
            pltpu.VMEM((shots, 2, cells_x + 8, cells_y), f32),
        ],
        compiler_params=params,
        cost_estimate=pl.CostEstimate(flops=10**7, bytes_accessed=6 * 10**6, transcendentals=0),
    )(
        local, adjoint_prev, now, courant, before, after, forward_snaps,
        traces, rec_x, rec_y, first_row, core, peak,
    )
    peaks = swapped(peak, ("shot", "brick"), beside)
    pieces = pl.pallas_call(
        join_kernel,
        out_shape=shape((parts // 2, cells_x + 1, rows_part, cells_y), f32),
        in_specs=vmem(3),
        out_specs=vmem(1)[0],
        compiler_params=params,
        cost_estimate=pl.CostEstimate(flops=10**5, bytes_accessed=10**6, transcendentals=0),
    )(image_halves, exchanged(image_halves), peaks)
    image_got = four_chips(pieces)

    gradient, sums = pl.pallas_call(
        gradient_kernel,
        out_shape=(shape((cells_x, rows_part, cells_y), f32), shape((len(along[0]), 1, 256), f32)),
        in_specs=vmem(4) + [smem],
        out_specs=tuple(vmem(2)),
        compiler_params=params,
        cost_estimate=pl.CostEstimate(flops=10**6, bytes_accessed=6 * 10**5, transcendentals=0),
    )(image_got, illum_part, water_rows, direction, offset[None])
    sums = fan(jnp.add, swapped(sums, "brick", along), len(across[0]))
    gradient, sums = pl.pallas_call(
        last_kernel,
        out_shape=(shape(gradient.shape, f32), shape((2,), f32)),
        in_specs=vmem(2),
        out_specs=(vmem(1)[0], smem),
        compiler_params=params,
        cost_estimate=pl.CostEstimate(flops=10**4, bytes_accessed=2 * 10**5, transcendentals=0),
    )(swapped(sums, ("shot", "brick"), across), gradient)
    return (gradient, sums)


def solution(mesh):
    in_specs = (
        P("shot", "brick", None, None),
        P("shot", "brick", None, None),
        P("shot", None, "brick", None, None),
        P("brick", None, None),
        P("shot", None, None),
        P("shot", None),
        P("shot", None),
        P("brick", None),
        P("brick", None, None),
    )
    out_specs = (P("brick", "shot", None), P())
    return jax.shard_map(
        per_device, mesh=mesh, in_specs=in_specs, out_specs=out_specs, check_vma=False
    )
```

```python
import functools

import jax
import jax.numpy as jnp
from jax import lax
from jax.experimental import pallas as pl
from jax.experimental.pallas import tpu as pltpu
from jax.sharding import PartitionSpec as P

far_coef = -1.0 / 12.0
near_coef = 4.0 / 3.0
receiver_depth = 2
water_level = 0.1
f32 = jnp.float32
bf16 = jnp.bfloat16


def vmem(count):
    return [pl.BlockSpec(memory_space=pltpu.VMEM)] * count


mib = 1024 * 1024
params = pltpu.CompilerParams(vmem_limit_bytes=16 * mib)


def band(size, center):
    gap = jnp.abs(
        lax.broadcasted_iota(jnp.int32, (size, size), 0)
        - lax.broadcasted_iota(jnp.int32, (size, size), 1)
    )
    weights = jnp.where(gap == 0, f32(center), f32(0.0))
    weights = jnp.where(gap == 1, f32(16.0), weights)
    return jnp.where(gap == 2, f32(-1.0), weights).astype(bf16)


def split_two(v):
    high = v.astype(bf16)
    return high, (v - high.astype(f32)).astype(bf16)


def in_plane(v, band_z, band_y):
    depth = v.shape[0]
    both = jnp.concatenate(split_two(v), axis=0)
    along_y = jnp.dot(both, band_y, preferred_element_type=f32)
    along_z = jnp.dot(band_z, both, preferred_element_type=f32)
    return along_z + along_y[:depth] + along_y[depth:]


def injected(trace, row_x, row_y, first_row, rows, cells_y):
    receivers = trace.shape[1]
    at_x = row_x == first_row + lax.broadcasted_iota(jnp.int32, (rows, receivers), 0)
    at_y = (row_y == lax.broadcasted_iota(jnp.int32, (cells_y, receivers), 0)).astype(f32)
    at_y = at_y.astype(bf16)
    rest = jnp.where(at_x, trace, f32(0.0))
    out = jnp.zeros((rows, cells_y), f32)
    for _ in range(3):
        part = rest.astype(bf16)
        rest = rest - part.astype(f32)
        out += lax.dot_general(
            part, at_y, (((1,), (1,)), ((), ())), preferred_element_type=f32
        )
    return out


def illum_kernel(snaps, core, first_row, first_depth, out):
    shots, steps, planes, depth, width = snaps.shape
    parts = 2 * out.shape[1]
    rows = depth // parts
    mine = core[0]
    for i in range(planes):
        total = None
        for s in range(shots):
            for k in range(steps):
                v = snaps[s, k, i].astype(f32)
                total = v * v if total is None else total + v * v
        for p in range(parts):
            slot = (mine + p % 2) % 2
            out[slot, p // 2, i] = total[p * rows : (p + 1) * rows]


def local_kernel(now, courant, out):
    shots, planes, depth, width = now.shape
    band_y = band(width, -90.0)
    band_z = jnp.concatenate([band(depth, 0.0)] * 2, axis=1)
    for s in range(shots):
        for i in range(planes):
            v = now[s, i]
            total = in_plane(v, band_z, band_y)
            for gap, weight in ((1, 16.0), (2, -1.0)):
                for j in (i - gap, i + gap):
                    if 0 <= j < planes:
                        total += weight * now[s, j]
            out[s, i] = 2.0 * v + courant[i] * (total * (1.0 / 12.0))


def edges_kernel(
    local, prev, now, courant, traces, rec_x, rec_y, head, tail, traces_out, x_out, y_out
):
    traces_out[...] = traces[...]
    x_out[...] = rec_x[...]
    y_out[...] = rec_y[...]
    shots, planes, depth, width = now.shape
    for side, start in ((head, 0), (tail, planes - 2)):
        for j in range(2):
            for s in range(shots):
                side[s, j] = local[s, start + j] - prev[s, start + j]
                side[shots + s, j] = now[s, start + j]
            side[2 * shots, j] = courant[start + j]


def image_kernel(
    local, prev, now, courant, before, after, snaps, traces, rec_x, rec_y, first_row, core, order,
    out, first, injections,
):
    shots, planes, depth, width = now.shape
    parts = 2 * out.shape[1]
    rows = depth // parts
    band_y = band(width, -90.0)
    band_z = jnp.concatenate([band(depth, 0.0)] * 2, axis=1)
    mine = core[0]
    last = planes - 1
    for s in range(shots):
        for k in range(2):
            injections[s, k] = injected(
                traces[s, k : k + 1], rec_x[s : s + 1], rec_y[s : s + 1],
                first_row[0] - 2, injections.shape[2], width,
            )
        first[s, 2] = local[s, 0] - prev[s, 0] + courant[0] * (
            far_coef * before[shots + s, 0] + near_coef * before[shots + s, 1]
        )
        first[s, 3] = local[s, 1] - prev[s, 1] + courant[1] * (far_coef * before[shots + s, 1])
        for i in range(2, planes - 2):
            first[s, i + 2] = local[s, i] - prev[s, i]
        first[s, planes] = local[s, last - 1] - prev[s, last - 1] + courant[last - 1] * (
            far_coef * after[shots + s, 0]
        )
        first[s, planes + 1] = local[s, last] - prev[s, last] + courant[last] * (
            near_coef * after[shots + s, 0] + far_coef * after[shots + s, 1]
        )
        first[s, 0] = before[s, 0] + before[2 * shots, 0] * (far_coef * now[s, 0])
        first[s, 1] = before[s, 1] + before[2 * shots, 1] * (
            near_coef * now[s, 0] + far_coef * now[s, 1]
        )
        first[s, planes + 2] = after[s, 0] + after[2 * shots, 0] * (
            near_coef * now[s, last] + far_coef * now[s, last - 1]
        )
        first[s, planes + 3] = after[s, 1] + after[2 * shots, 1] * (far_coef * now[s, last])
        for i in range(planes + 4):
            first[s, i, receiver_depth : receiver_depth + 1] += injections[s, 0, i : i + 1]
    at_level = (
        lax.broadcasted_iota(jnp.int32, (depth, width), 0) == receiver_depth
    )
    for i in range(planes):
        image = None
        for s in range(shots):
            v = first[s, i + 2]
            total = in_plane(v, band_z, band_y)
            total += 16.0 * (first[s, i + 1] + first[s, i + 3])
            total -= first[s, i] + first[s, i + 4]
            second = 2.0 * v - now[s, i] + courant[i] * (total * (1.0 / 12.0))
            second += jnp.where(at_level, injections[s, 1, i + 2 : i + 3], f32(0.0))
            term = snaps[s, 0, i].astype(f32) * v + snaps[s, 1, i].astype(f32) * second
            image = term if image is None else image + term
        for p in range(parts):
            slot = (mine + p % 2) % 2
            out[slot, p // 2, i] = image[p * rows : (p + 1) * rows]


def folded(line, combine):
    out = line[:, :128]
    for j in range(128, line.shape[1], 128):
        out = combine(out, line[:, j : j + 128])
    return out


def peak_kernel(got, part, peak):
    total = got[0]
    for c in range(1, got.shape[0]):
        total = total + got[c]
    part[...] = total
    top = folded(jnp.max(jnp.max(total, axis=0), axis=0, keepdims=True), jnp.maximum)
    for n in range(peak.shape[0]):
        peak[n] = top


def fan_kernel(combine, got, out):
    total = got[0]
    for n in range(1, got.shape[0]):
        total = combine(total, got[n])
    for n in range(out.shape[0]):
        out[n] = total


def join_kernel(halves, received, peaks, out):
    chips, planes, rows, width = received.shape
    for c in range(chips):
        for i in range(planes):
            out[c, i] = halves[0, c, i] + received[c, i]
    top = jnp.broadcast_to(jnp.max(peaks[...], axis=0), (rows, 128))
    for c in range(chips):
        for j in range(0, width, 128):
            out[c, planes, :, j : j + 128] = top


def gradient_kernel(got, illum, water, direction, first_depth, gradient, sums):
    planes, rows, width = illum.shape
    top = got[0, planes]
    for c in range(1, got.shape[0]):
        top = jnp.maximum(top, got[c, planes])
    peak = jnp.max(top)
    span = pl.ds(pl.multiple_of(first_depth[0], rows), rows)
    depth = first_depth[0] + lax.broadcasted_iota(jnp.int32, (rows, width), 0)
    square = jnp.zeros((rows, width), f32)
    along = jnp.zeros((rows, width), f32)
    for i in range(planes):
        image = got[0, i]
        for c in range(1, got.shape[0]):
            image = image + got[c, i]
        value = image / (illum[i] + water_level * peak)
        value = jnp.where(depth >= water[i : i + 1], value, f32(0.0))
        gradient[i] = value
        square += value * value
        along += value * direction[i, span]
    for k, total in ((0, square), (1, along)):
        line = folded(jnp.sum(total, axis=0, keepdims=True), jnp.add)
        for n in range(sums.shape[0]):
            sums[n, :, k * 128 : (k + 1) * 128] = line


def last_kernel(got, value, gradient, sums):
    gradient[...] = value[...]
    total = got[0]
    for n in range(1, got.shape[0]):
        total = total + got[n]
    sums[0] = jnp.sum(total[:, :128])
    sums[1] = jnp.sum(total[:, 128:])


def to_next(cells):
    count = lax.axis_size("brick")
    return lax.ppermute(cells, "brick", [(i, i + 1) for i in range(count - 1)])


def to_previous(cells):
    count = lax.axis_size("brick")
    return lax.ppermute(cells, "brick", [(i + 1, i) for i in range(count - 1)])


def swapped(copies, axis, groups):
    return lax.all_to_all(copies, axis, 0, 0, axis_index_groups=groups, tiled=True)


def fan(combine, got, count):
    return pl.pallas_call(
        functools.partial(fan_kernel, combine),
        out_shape=jax.ShapeDtypeStruct((count,) + got.shape[1:], f32),
        in_specs=vmem(1),
        out_specs=vmem(1)[0],
        compiler_params=params,
        cost_estimate=pl.CostEstimate(flops=10**4, bytes_accessed=10**4, transcendentals=0),
    )(got)


def exchanged(halves):
    parts = lax.axis_size("shot")
    return lax.ppermute(halves[1], "shot", [(i, i ^ 1) for i in range(parts)])


def four_chips(pieces):
    parts = lax.axis_size("shot")
    groups = [[2 * c + core for c in range(parts // 2)] for core in range(2)]
    return lax.all_to_all(pieces, "shot", 0, 0, axis_index_groups=groups, tiled=True)


def per_device(
    adjoint_prev, adjoint_now, forward_snaps, courant, traces, rec_x, rec_y, water_rows, direction
):
    now = adjoint_now
    shots, cells_x, depth_cells, cells_y = now.shape
    parts = lax.axis_size("shot")
    bricks = lax.axis_size("brick")
    rows_part = depth_cells // parts
    columns = 4
    along = [[g + columns * i for i in range(bricks // columns)] for g in range(columns)]
    across = [
        [bricks * s + columns * g + i for s in range(parts) for i in range(columns)]
        for g in range(bricks // columns)
    ]
    beside = [
        [bricks * (2 * c + core) + columns * g + i for core in range(2) for i in range(columns)]
        for c in range(parts // 2)
        for g in range(bricks // columns)
    ]
    shot = lax.axis_index("shot")
    first_row = (lax.axis_index("brick") * cells_x).astype(jnp.int32)[None]
    core = (shot % 2).astype(jnp.int32)[None]
    offset = (shot * rows_part).astype(jnp.int32)
    smem = pl.BlockSpec(memory_space=pltpu.SMEM)
    shape = jax.ShapeDtypeStruct
    halves_shape = shape((2, parts // 2, cells_x, rows_part, cells_y), f32)

    illum_halves = pl.pallas_call(
        illum_kernel,
        out_shape=halves_shape,
        in_specs=vmem(1) + [smem, smem, smem],
        out_specs=vmem(1)[0],
        compiler_params=params,
        cost_estimate=pl.CostEstimate(flops=10**6, bytes_accessed=2 * 10**6, transcendentals=0),
    )(forward_snaps, core, first_row, offset[None])
    illum_mine = illum_halves[0] + exchanged(illum_halves)
    illum_got = four_chips(illum_mine)

    illum_part, own_peak = pl.pallas_call(
        peak_kernel,
        out_shape=(
            shape((cells_x, rows_part, cells_y), f32),
            shape((len(along[0]), 1, 128), f32),
        ),
        in_specs=vmem(1),
        out_specs=tuple(vmem(2)),
        compiler_params=params,
        cost_estimate=pl.CostEstimate(flops=10**5, bytes_accessed=4 * 10**5, transcendentals=0),
    )(illum_got)
    peak = fan(jnp.maximum, swapped(own_peak, "brick", along), len(beside[0]))

    side_shape = shape((2 * shots + 1, 2, depth_cells, cells_y), f32)
    local = pl.pallas_call(
        local_kernel,
        out_shape=shape(now.shape, f32),
        in_specs=vmem(2),
        out_specs=vmem(1)[0],
        compiler_params=params,
        cost_estimate=pl.CostEstimate(flops=10**7, bytes_accessed=4 * 10**6, transcendentals=0),
    )(now, courant)
    head, tail, traces, rec_x, rec_y = pl.pallas_call(
        edges_kernel,
        out_shape=(
            side_shape,
            side_shape,
            shape(traces.shape, f32),
            shape(rec_x.shape, jnp.int32),
            shape(rec_y.shape, jnp.int32),
        ),
        in_specs=vmem(7),
        out_specs=tuple(vmem(5)),
        compiler_params=params,
        cost_estimate=pl.CostEstimate(flops=10**5, bytes_accessed=10**6, transcendentals=0),
    )(local, adjoint_prev, now, courant, traces, rec_x, rec_y)
    before = to_next(tail)
    after = to_previous(head)

    image_halves = pl.pallas_call(
        image_kernel,
        out_shape=halves_shape,
        in_specs=vmem(10) + [smem, smem] + vmem(1),
        out_specs=vmem(1)[0],
        scratch_shapes=[
            pltpu.VMEM((shots, cells_x + 4, depth_cells, cells_y), f32),
            pltpu.VMEM((shots, 2, cells_x + 8, cells_y), f32),
        ],
        compiler_params=params,
        cost_estimate=pl.CostEstimate(flops=10**7, bytes_accessed=6 * 10**6, transcendentals=0),
    )(
        local, adjoint_prev, now, courant, before, after, forward_snaps,
        traces, rec_x, rec_y, first_row, core, peak,
    )
    peaks = swapped(peak, ("shot", "brick"), beside)
    pieces = pl.pallas_call(
        join_kernel,
        out_shape=shape((parts // 2, cells_x + 1, rows_part, cells_y), f32),
        in_specs=vmem(3),
        out_specs=vmem(1)[0],
        compiler_params=params,
        cost_estimate=pl.CostEstimate(flops=10**5, bytes_accessed=10**6, transcendentals=0),
    )(image_halves, exchanged(image_halves), peaks)
    image_got = four_chips(pieces)

    gradient, sums = pl.pallas_call(
        gradient_kernel,
        out_shape=(shape((cells_x, rows_part, cells_y), f32), shape((len(along[0]), 1, 256), f32)),
        in_specs=vmem(4) + [smem],
        out_specs=tuple(vmem(2)),
        compiler_params=params,
        cost_estimate=pl.CostEstimate(flops=10**6, bytes_accessed=6 * 10**5, transcendentals=0),
    )(image_got, illum_part, water_rows, direction, offset[None])
    sums = fan(jnp.add, swapped(sums, "brick", along), len(across[0]))
    gradient, sums = pl.pallas_call(
        last_kernel,
        out_shape=(shape(gradient.shape, f32), shape((2,), f32)),
        in_specs=vmem(2),
        out_specs=(vmem(1)[0], smem),
        compiler_params=params,
        cost_estimate=pl.CostEstimate(flops=10**4, bytes_accessed=2 * 10**5, transcendentals=0),
    )(swapped(sums, ("shot", "brick"), across), gradient)
    return (gradient, sums)


def solution(mesh):
    in_specs = (
        P("shot", "brick", None, None),
        P("shot", "brick", None, None),
        P("shot", None, "brick", None, None),
        P("brick", None, None),
        P("shot", None, None),
        P("shot", None),
        P("shot", None),
        P("brick", None),
        P("brick", None, None),
    )
    out_specs = (P("brick", "shot", None), P())
    return jax.shard_map(
        per_device, mesh=mesh, in_specs=in_specs, out_specs=out_specs, check_vma=False
    )
```

```python
import functools

import jax
import jax.numpy as jnp
from jax import lax
from jax.experimental import pallas as pl
from jax.experimental.pallas import tpu as pltpu
from jax.sharding import PartitionSpec as P

far_coef = -1.0 / 12.0
near_coef = 4.0 / 3.0
receiver_depth = 2
water_level = 0.1
f32 = jnp.float32
bf16 = jnp.bfloat16


def vmem(count):
    return [pl.BlockSpec(memory_space=pltpu.VMEM)] * count


mib = 1024 * 1024
params = pltpu.CompilerParams(vmem_limit_bytes=16 * mib)


def band(size, center):
    gap = jnp.abs(
        lax.broadcasted_iota(jnp.int32, (size, size), 0)
        - lax.broadcasted_iota(jnp.int32, (size, size), 1)
    )
    weights = jnp.where(gap == 0, f32(center), f32(0.0))
    weights = jnp.where(gap == 1, f32(16.0), weights)
    return jnp.where(gap == 2, f32(-1.0), weights).astype(bf16)


def split_two(v):
    high = v.astype(bf16)
    return high, (v - high.astype(f32)).astype(bf16)


def in_plane(v, band_z, band_y):
    depth = v.shape[0]
    both = jnp.concatenate(split_two(v), axis=0)
    along_y = jnp.dot(both, band_y, preferred_element_type=f32)
    along_z = jnp.dot(band_z, both, preferred_element_type=f32)
    return along_z + along_y[:depth] + along_y[depth:]


def injected(trace, row_x, row_y, first_row, rows, cells_y):
    receivers = trace.shape[1]
    at_x = row_x == first_row + lax.broadcasted_iota(jnp.int32, (rows, receivers), 0)
    at_y = (row_y == lax.broadcasted_iota(jnp.int32, (cells_y, receivers), 0)).astype(f32)
    at_y = at_y.astype(bf16)
    rest = jnp.where(at_x, trace, f32(0.0))
    out = jnp.zeros((rows, cells_y), f32)
    for _ in range(3):
        part = rest.astype(bf16)
        rest = rest - part.astype(f32)
        out += lax.dot_general(
            part, at_y, (((1,), (1,)), ((), ())), preferred_element_type=f32
        )
    return out


def illum_kernel(snaps, core, first_row, first_depth, out):
    shots, steps, planes, depth, width = snaps.shape
    parts = 2 * out.shape[1]
    rows = depth // parts
    mine = core[0]
    for i in range(planes):
        total = None
        for s in range(shots):
            for k in range(steps):
                v = snaps[s, k, i].astype(f32)
                total = v * v if total is None else total + v * v
        for p in range(parts):
            slot = (mine + p % 2) % 2
            out[slot, p // 2, i] = total[p * rows : (p + 1) * rows]


def local_kernel(now, courant, out):
    shots, planes, depth, width = now.shape
    band_y = band(width, -90.0)
    band_z = jnp.concatenate([band(depth, 0.0)] * 2, axis=1)
    for s in range(shots):
        for i in range(planes):
            v = now[s, i]
            total = in_plane(v, band_z, band_y)
            for gap, weight in ((1, 16.0), (2, -1.0)):
                for j in (i - gap, i + gap):
                    if 0 <= j < planes:
                        total += weight * now[s, j]
            out[s, i] = 2.0 * v + courant[i] * (total * (1.0 / 12.0))


def edges_kernel(
    local, prev, now, courant, traces, rec_x, rec_y, head, tail, traces_out, x_out, y_out
):
    traces_out[...] = traces[...]
    x_out[...] = rec_x[...]
    y_out[...] = rec_y[...]
    shots, planes, depth, width = now.shape
    for side, start in ((head, 0), (tail, planes - 2)):
        for j in range(2):
            for s in range(shots):
                side[s, j] = local[s, start + j] - prev[s, start + j]
                side[shots + s, j] = now[s, start + j]
            side[2 * shots, j] = courant[start + j]


def image_kernel(
    local, prev, now, courant, before, after, snaps, traces, rec_x, rec_y, first_row, core, order,
    out, first, injections,
):
    shots, planes, depth, width = now.shape
    parts = 2 * out.shape[1]
    rows = depth // parts
    band_y = band(width, -90.0)
    band_z = jnp.concatenate([band(depth, 0.0)] * 2, axis=1)
    mine = core[0]
    last = planes - 1
    for s in range(shots):
        for k in range(2):
            injections[s, k] = injected(
                traces[s, k : k + 1], rec_x[s : s + 1], rec_y[s : s + 1],
                first_row[0] - 2, injections.shape[2], width,
            )
        first[s, 2] = local[s, 0] - prev[s, 0] + courant[0] * (
            far_coef * before[shots + s, 0] + near_coef * before[shots + s, 1]
        )
        first[s, 3] = local[s, 1] - prev[s, 1] + courant[1] * (far_coef * before[shots + s, 1])
        for i in range(2, planes - 2):
            first[s, i + 2] = local[s, i] - prev[s, i]
        first[s, planes] = local[s, last - 1] - prev[s, last - 1] + courant[last - 1] * (
            far_coef * after[shots + s, 0]
        )
        first[s, planes + 1] = local[s, last] - prev[s, last] + courant[last] * (
            near_coef * after[shots + s, 0] + far_coef * after[shots + s, 1]
        )
        first[s, 0] = before[s, 0] + before[2 * shots, 0] * (far_coef * now[s, 0])
        first[s, 1] = before[s, 1] + before[2 * shots, 1] * (
            near_coef * now[s, 0] + far_coef * now[s, 1]
        )
        first[s, planes + 2] = after[s, 0] + after[2 * shots, 0] * (
            near_coef * now[s, last] + far_coef * now[s, last - 1]
        )
        first[s, planes + 3] = after[s, 1] + after[2 * shots, 1] * (far_coef * now[s, last])
        for i in range(planes + 4):
            first[s, i, receiver_depth : receiver_depth + 1] += injections[s, 0, i : i + 1]
    at_level = (
        lax.broadcasted_iota(jnp.int32, (depth, width), 0) == receiver_depth
    )
    for i in range(planes):
        image = None
        for s in range(shots):
            v = first[s, i + 2]
            total = in_plane(v, band_z, band_y)
            total += 16.0 * (first[s, i + 1] + first[s, i + 3])
            total -= first[s, i] + first[s, i + 4]
            second = 2.0 * v - now[s, i] + courant[i] * (total * (1.0 / 12.0))
            second += jnp.where(at_level, injections[s, 1, i + 2 : i + 3], f32(0.0))
            term = snaps[s, 0, i].astype(f32) * v + snaps[s, 1, i].astype(f32) * second
            image = term if image is None else image + term
        for p in range(parts):
            slot = (mine + p % 2) % 2
            out[slot, p // 2, i] = image[p * rows : (p + 1) * rows]


def folded(line, combine):
    out = line[:, :128]
    for j in range(128, line.shape[1], 128):
        out = combine(out, line[:, j : j + 128])
    return out


def peak_kernel(got, part, peak):
    total = got[0]
    for c in range(1, got.shape[0]):
        total = total + got[c]
    part[...] = total
    top = folded(jnp.max(jnp.max(total, axis=0), axis=0, keepdims=True), jnp.maximum)
    for n in range(peak.shape[0]):
        peak[n] = top


def fan_kernel(combine, got, out):
    total = got[0]
    for n in range(1, got.shape[0]):
        total = combine(total, got[n])
    for n in range(out.shape[0]):
        out[n] = total


def join_kernel(halves, received, peaks, out):
    chips, planes, rows, width = received.shape
    for c in range(chips):
        for i in range(planes):
            out[c, i] = halves[0, c, i] + received[c, i]
    top = jnp.broadcast_to(jnp.max(peaks[...], axis=0), (rows, 128))
    for c in range(chips):
        for j in range(0, width, 128):
            out[c, planes, :, j : j + 128] = top


def gradient_kernel(got, illum, water, direction, first_depth, gradient, sums):
    planes, rows, width = illum.shape
    top = got[0, planes]
    for c in range(1, got.shape[0]):
        top = jnp.maximum(top, got[c, planes])
    peak = jnp.max(top)
    span = pl.ds(pl.multiple_of(first_depth[0], rows), rows)
    depth = first_depth[0] + lax.broadcasted_iota(jnp.int32, (rows, width), 0)
    square = jnp.zeros((rows, width), f32)
    along = jnp.zeros((rows, width), f32)
    for i in range(planes):
        image = got[0, i]
        for c in range(1, got.shape[0]):
            image = image + got[c, i]
        value = image / (illum[i] + water_level * peak)
        value = jnp.where(depth >= water[i : i + 1], value, f32(0.0))
        gradient[i] = value
        square += value * value
        along += value * direction[i, span]
    square, along = (folded(total, jnp.add) for total in (square, along))
    square, along = (total + pltpu.roll(total, 64, 1) for total in (square, along))
    lane = lax.broadcasted_iota(jnp.int32, square.shape, 1)
    line = jnp.sum(jnp.where(lane < 64, square, along), axis=0, keepdims=True)
    for n in range(sums.shape[0]):
        sums[n] = line


def last_kernel(got, value, gradient, sums):
    gradient[...] = value[...]
    total = got[0]
    for n in range(1, got.shape[0]):
        total = total + got[n]
    lane = lax.broadcasted_iota(jnp.int32, total.shape, 1)
    sums[0] = jnp.sum(jnp.where(lane < 64, total, f32(0.0)))
    sums[1] = jnp.sum(jnp.where(lane < 64, f32(0.0), total))


def to_next(cells):
    count = lax.axis_size("brick")
    return lax.ppermute(cells, "brick", [(i, i + 1) for i in range(count - 1)])


def to_previous(cells):
    count = lax.axis_size("brick")
    return lax.ppermute(cells, "brick", [(i + 1, i) for i in range(count - 1)])


def swapped(copies, axis, groups):
    return lax.all_to_all(copies, axis, 0, 0, axis_index_groups=groups, tiled=True)


def fan(combine, got, count):
    return pl.pallas_call(
        functools.partial(fan_kernel, combine),
        out_shape=jax.ShapeDtypeStruct((count,) + got.shape[1:], f32),
        in_specs=vmem(1),
        out_specs=vmem(1)[0],
        compiler_params=params,
        cost_estimate=pl.CostEstimate(flops=10**4, bytes_accessed=10**4, transcendentals=0),
    )(got)


def exchanged(halves):
    parts = lax.axis_size("shot")
    return lax.ppermute(halves[1], "shot", [(i, i ^ 1) for i in range(parts)])


def four_chips(pieces):
    parts = lax.axis_size("shot")
    groups = [[2 * c + core for c in range(parts // 2)] for core in range(2)]
    return lax.all_to_all(pieces, "shot", 0, 0, axis_index_groups=groups, tiled=True)


def per_device(
    adjoint_prev, adjoint_now, forward_snaps, courant, traces, rec_x, rec_y, water_rows, direction
):
    now = adjoint_now
    shots, cells_x, depth_cells, cells_y = now.shape
    parts = lax.axis_size("shot")
    bricks = lax.axis_size("brick")
    rows_part = depth_cells // parts
    columns = 4
    along = [[g + columns * i for i in range(bricks // columns)] for g in range(columns)]
    across = [
        [bricks * s + columns * g + i for s in range(parts) for i in range(columns)]
        for g in range(bricks // columns)
    ]
    beside = [
        [bricks * (2 * c + core) + columns * g + i for core in range(2) for i in range(columns)]
        for c in range(parts // 2)
        for g in range(bricks // columns)
    ]
    shot = lax.axis_index("shot")
    first_row = (lax.axis_index("brick") * cells_x).astype(jnp.int32)[None]
    core = (shot % 2).astype(jnp.int32)[None]
    offset = (shot * rows_part).astype(jnp.int32)
    smem = pl.BlockSpec(memory_space=pltpu.SMEM)
    shape = jax.ShapeDtypeStruct
    halves_shape = shape((2, parts // 2, cells_x, rows_part, cells_y), f32)

    illum_halves = pl.pallas_call(
        illum_kernel,
        out_shape=halves_shape,
        in_specs=vmem(1) + [smem, smem, smem],
        out_specs=vmem(1)[0],
        compiler_params=params,
        cost_estimate=pl.CostEstimate(flops=10**6, bytes_accessed=2 * 10**6, transcendentals=0),
    )(forward_snaps, core, first_row, offset[None])
    illum_mine = illum_halves[0] + exchanged(illum_halves)
    illum_got = four_chips(illum_mine)

    illum_part, own_peak = pl.pallas_call(
        peak_kernel,
        out_shape=(
            shape((cells_x, rows_part, cells_y), f32),
            shape((len(along[0]), 1, 128), f32),
        ),
        in_specs=vmem(1),
        out_specs=tuple(vmem(2)),
        compiler_params=params,
        cost_estimate=pl.CostEstimate(flops=10**5, bytes_accessed=4 * 10**5, transcendentals=0),
    )(illum_got)
    peak = fan(jnp.maximum, swapped(own_peak, "brick", along), len(beside[0]))

    side_shape = shape((2 * shots + 1, 2, depth_cells, cells_y), f32)
    local = pl.pallas_call(
        local_kernel,
        out_shape=shape(now.shape, f32),
        in_specs=vmem(2),
        out_specs=vmem(1)[0],
        compiler_params=params,
        cost_estimate=pl.CostEstimate(flops=10**7, bytes_accessed=4 * 10**6, transcendentals=0),
    )(now, courant)
    head, tail, traces, rec_x, rec_y = pl.pallas_call(
        edges_kernel,
        out_shape=(
            side_shape,
            side_shape,
            shape(traces.shape, f32),
            shape(rec_x.shape, jnp.int32),
            shape(rec_y.shape, jnp.int32),
        ),
        in_specs=vmem(7),
        out_specs=tuple(vmem(5)),
        compiler_params=params,
        cost_estimate=pl.CostEstimate(flops=10**5, bytes_accessed=10**6, transcendentals=0),
    )(local, adjoint_prev, now, courant, traces, rec_x, rec_y)
    before = to_next(tail)
    after = to_previous(head)

    image_halves = pl.pallas_call(
        image_kernel,
        out_shape=halves_shape,
        in_specs=vmem(10) + [smem, smem] + vmem(1),
        out_specs=vmem(1)[0],
        scratch_shapes=[
            pltpu.VMEM((shots, cells_x + 4, depth_cells, cells_y), f32),
            pltpu.VMEM((shots, 2, cells_x + 8, cells_y), f32),
        ],
        compiler_params=params,
        cost_estimate=pl.CostEstimate(flops=10**7, bytes_accessed=6 * 10**6, transcendentals=0),
    )(
        local, adjoint_prev, now, courant, before, after, forward_snaps,
        traces, rec_x, rec_y, first_row, core, peak,
    )
    peaks = swapped(peak, ("shot", "brick"), beside)
    pieces = pl.pallas_call(
        join_kernel,
        out_shape=shape((parts // 2, cells_x + 1, rows_part, cells_y), f32),
        in_specs=vmem(3),
        out_specs=vmem(1)[0],
        compiler_params=params,
        cost_estimate=pl.CostEstimate(flops=10**5, bytes_accessed=10**6, transcendentals=0),
    )(image_halves, exchanged(image_halves), peaks)
    image_got = four_chips(pieces)

    gradient, sums = pl.pallas_call(
        gradient_kernel,
        out_shape=(shape((cells_x, rows_part, cells_y), f32), shape((len(along[0]), 1, 128), f32)),
        in_specs=vmem(4) + [smem],
        out_specs=tuple(vmem(2)),
        compiler_params=params,
        cost_estimate=pl.CostEstimate(flops=10**6, bytes_accessed=6 * 10**5, transcendentals=0),
    )(image_got, illum_part, water_rows, direction, offset[None])
    sums = fan(jnp.add, swapped(sums, "brick", along), len(across[0]))
    gradient, sums = pl.pallas_call(
        last_kernel,
        out_shape=(shape(gradient.shape, f32), shape((2,), f32)),
        in_specs=vmem(2),
        out_specs=(vmem(1)[0], smem),
        compiler_params=params,
        cost_estimate=pl.CostEstimate(flops=10**4, bytes_accessed=2 * 10**5, transcendentals=0),
    )(swapped(sums, ("shot", "brick"), across), gradient)
    return (gradient, sums)


def solution(mesh):
    in_specs = (
        P("shot", "brick", None, None),
        P("shot", "brick", None, None),
        P("shot", None, "brick", None, None),
        P("brick", None, None),
        P("shot", None, None),
        P("shot", None),
        P("shot", None),
        P("brick", None),
        P("brick", None, None),
    )
    out_specs = (P("brick", "shot", None), P())
    return jax.shard_map(
        per_device, mesh=mesh, in_specs=in_specs, out_specs=out_specs, check_vma=False
    )
```

```python
import functools

import jax
import jax.numpy as jnp
from jax import lax
from jax.experimental import pallas as pl
from jax.experimental.pallas import tpu as pltpu
from jax.sharding import PartitionSpec as P

far_coef = -1.0 / 12.0
near_coef = 4.0 / 3.0
receiver_depth = 2
water_level = 0.1
f32 = jnp.float32
bf16 = jnp.bfloat16


def vmem(count):
    return [pl.BlockSpec(memory_space=pltpu.VMEM)] * count


mib = 1024 * 1024
params = pltpu.CompilerParams(vmem_limit_bytes=16 * mib)


def band(size, center):
    gap = jnp.abs(
        lax.broadcasted_iota(jnp.int32, (size, size), 0)
        - lax.broadcasted_iota(jnp.int32, (size, size), 1)
    )
    weights = jnp.where(gap == 0, f32(center), f32(0.0))
    weights = jnp.where(gap == 1, f32(16.0), weights)
    return jnp.where(gap == 2, f32(-1.0), weights).astype(bf16)


def split_two(v):
    high = v.astype(bf16)
    return high, (v - high.astype(f32)).astype(bf16)


def in_plane(v, band_z, band_y):
    depth = v.shape[0]
    both = jnp.concatenate(split_two(v), axis=0)
    along_y = jnp.dot(both, band_y, preferred_element_type=f32)
    along_z = jnp.dot(band_z, both, preferred_element_type=f32)
    return along_z + along_y[:depth] + along_y[depth:]


def injected(trace, row_x, row_y, first_row, rows, cells_y):
    receivers = trace.shape[1]
    at_x = row_x == first_row + lax.broadcasted_iota(jnp.int32, (rows, receivers), 0)
    at_y = (row_y == lax.broadcasted_iota(jnp.int32, (cells_y, receivers), 0)).astype(f32)
    at_y = at_y.astype(bf16)
    rest = jnp.where(at_x, trace, f32(0.0))
    out = jnp.zeros((rows, cells_y), f32)
    for _ in range(3):
        part = rest.astype(bf16)
        rest = rest - part.astype(f32)
        out += lax.dot_general(
            part, at_y, (((1,), (1,)), ((), ())), preferred_element_type=f32
        )
    return out


def illum_kernel(snaps, core, first_row, first_depth, out):
    shots, steps, planes, depth, width = snaps.shape
    parts = 2 * out.shape[1]
    rows = depth // parts
    mine = core[0]
    for i in range(planes):
        total = None
        for s in range(shots):
            for k in range(steps):
                v = snaps[s, k, i].astype(f32)
                total = v * v if total is None else total + v * v
        for p in range(parts):
            slot = (mine + p % 2) % 2
            out[slot, p // 2, i] = total[p * rows : (p + 1) * rows]


def local_kernel(now, courant, out):
    shots, planes, depth, width = now.shape
    band_y = band(width, -90.0)
    band_z = jnp.concatenate([band(depth, 0.0)] * 2, axis=1)
    for s in range(shots):
        for i in range(planes):
            v = now[s, i]
            total = in_plane(v, band_z, band_y)
            for gap, weight in ((1, 16.0), (2, -1.0)):
                for j in (i - gap, i + gap):
                    if 0 <= j < planes:
                        total += weight * now[s, j]
            out[s, i] = 2.0 * v + courant[i] * (total * (1.0 / 12.0))


def edges_kernel(
    local, prev, now, courant, traces, rec_x, rec_y, head, tail, traces_out, x_out, y_out
):
    traces_out[...] = traces[...]
    x_out[...] = rec_x[...]
    y_out[...] = rec_y[...]
    shots, planes, depth, width = now.shape
    for side, start in ((head, 0), (tail, planes - 2)):
        for j in range(2):
            for s in range(shots):
                side[s, j] = local[s, start + j] - prev[s, start + j]
                side[shots + s, j] = now[s, start + j]
            side[2 * shots, j] = courant[start + j]


def image_kernel(
    local, prev, now, courant, before, after, snaps, traces, rec_x, rec_y, first_row, core, order,
    out, first, injections,
):
    shots, planes, depth, width = now.shape
    parts = 2 * out.shape[1]
    rows = depth // parts
    band_y = band(width, -90.0)
    band_z = jnp.concatenate([band(depth, 0.0)] * 2, axis=1)
    mine = core[0]
    last = planes - 1
    for s in range(shots):
        for k in range(2):
            injections[s, k] = injected(
                traces[s, k : k + 1], rec_x[s : s + 1], rec_y[s : s + 1],
                first_row[0] - 2, injections.shape[2], width,
            )
        first[s, 2] = local[s, 0] - prev[s, 0] + courant[0] * (
            far_coef * before[shots + s, 0] + near_coef * before[shots + s, 1]
        )
        first[s, 3] = local[s, 1] - prev[s, 1] + courant[1] * (far_coef * before[shots + s, 1])
        for i in range(2, planes - 2):
            first[s, i + 2] = local[s, i] - prev[s, i]
        first[s, planes] = local[s, last - 1] - prev[s, last - 1] + courant[last - 1] * (
            far_coef * after[shots + s, 0]
        )
        first[s, planes + 1] = local[s, last] - prev[s, last] + courant[last] * (
            near_coef * after[shots + s, 0] + far_coef * after[shots + s, 1]
        )
        first[s, 0] = before[s, 0] + before[2 * shots, 0] * (far_coef * now[s, 0])
        first[s, 1] = before[s, 1] + before[2 * shots, 1] * (
            near_coef * now[s, 0] + far_coef * now[s, 1]
        )
        first[s, planes + 2] = after[s, 0] + after[2 * shots, 0] * (
            near_coef * now[s, last] + far_coef * now[s, last - 1]
        )
        first[s, planes + 3] = after[s, 1] + after[2 * shots, 1] * (far_coef * now[s, last])
        for i in range(planes + 4):
            first[s, i, receiver_depth : receiver_depth + 1] += injections[s, 0, i : i + 1]
    at_level = (
        lax.broadcasted_iota(jnp.int32, (depth, width), 0) == receiver_depth
    )
    for i in range(planes):
        image = None
        for s in range(shots):
            v = first[s, i + 2]
            total = in_plane(v, band_z, band_y)
            total += 16.0 * (first[s, i + 1] + first[s, i + 3])
            total -= first[s, i] + first[s, i + 4]
            second = 2.0 * v - now[s, i] + courant[i] * (total * (1.0 / 12.0))
            second += jnp.where(at_level, injections[s, 1, i + 2 : i + 3], f32(0.0))
            term = snaps[s, 0, i].astype(f32) * v + snaps[s, 1, i].astype(f32) * second
            image = term if image is None else image + term
        for p in range(parts):
            slot = (mine + p % 2) % 2
            out[slot, p // 2, i] = image[p * rows : (p + 1) * rows]


def folded(line, combine):
    out = line[:, :128]
    for j in range(128, line.shape[1], 128):
        out = combine(out, line[:, j : j + 128])
    return out


def peak_kernel(got, part, peak):
    total = got[0]
    for c in range(1, got.shape[0]):
        total = total + got[c]
    part[...] = total
    top = folded(jnp.max(jnp.max(total, axis=0), axis=0, keepdims=True), jnp.maximum)
    for n in range(peak.shape[0]):
        peak[n] = top


def fan_kernel(combine, got, out):
    total = got[0]
    for n in range(1, got.shape[0]):
        total = combine(total, got[n])
    for n in range(out.shape[0]):
        out[n] = total


def join_kernel(halves, received, peaks, out):
    chips, planes, rows, width = received.shape
    for c in range(chips):
        for i in range(planes):
            out[c, i] = halves[0, c, i] + received[c, i]
    top = jnp.broadcast_to(jnp.max(peaks[...], axis=0), (rows, 128))
    for c in range(chips):
        for j in range(0, width, 128):
            out[c, planes, :, j : j + 128] = top


def gradient_kernel(got, illum, water, direction, first_depth, gradient, sums):
    planes, rows, width = illum.shape
    top = got[0, planes]
    for c in range(1, got.shape[0]):
        top = jnp.maximum(top, got[c, planes])
    peak = jnp.max(top)
    span = pl.ds(pl.multiple_of(first_depth[0], rows), rows)
    depth = first_depth[0] + lax.broadcasted_iota(jnp.int32, (rows, width), 0)
    square = jnp.zeros((rows, width), f32)
    along = jnp.zeros((rows, width), f32)
    for i in range(planes):
        image = got[0, i]
        for c in range(1, got.shape[0]):
            image = image + got[c, i]
        value = image / (illum[i] + water_level * peak)
        value = jnp.where(depth >= water[i : i + 1], value, f32(0.0))
        gradient[i] = value
        square += value * value
        along += value * direction[i, span]
    for k, total in ((0, square), (1, along)):
        line = folded(jnp.sum(total, axis=0, keepdims=True), jnp.add)
        for n in range(sums.shape[0]):
            sums[n, :, k * 128 : (k + 1) * 128] = line


def last_kernel(got, value, gradient, sums):
    gradient[...] = value[...]
    total = got[0]
    for n in range(1, got.shape[0]):
        total = total + got[n]
    sums[0] = jnp.sum(total[:, :128])
    sums[1] = jnp.sum(total[:, 128:])


def to_next(cells):
    count = lax.axis_size("brick")
    return lax.ppermute(cells, "brick", [(i, i + 1) for i in range(count - 1)])


def to_previous(cells):
    count = lax.axis_size("brick")
    return lax.ppermute(cells, "brick", [(i + 1, i) for i in range(count - 1)])


def swapped(copies, axis, groups):
    return lax.all_to_all(copies, axis, 0, 0, axis_index_groups=groups, tiled=True)


def fan(combine, got, count):
    return pl.pallas_call(
        functools.partial(fan_kernel, combine),
        out_shape=jax.ShapeDtypeStruct((count,) + got.shape[1:], f32),
        in_specs=vmem(1),
        out_specs=vmem(1)[0],
        compiler_params=params,
        cost_estimate=pl.CostEstimate(flops=10**4, bytes_accessed=10**4, transcendentals=0),
    )(got)


def exchanged(halves):
    parts = lax.axis_size("shot")
    return lax.ppermute(halves[1], "shot", [(i, i ^ 1) for i in range(parts)])


def four_chips(pieces):
    parts = lax.axis_size("shot")
    groups = [[2 * c + core for c in range(parts // 2)] for core in range(2)]
    return lax.all_to_all(pieces, "shot", 0, 0, axis_index_groups=groups, tiled=True)


def per_device(
    adjoint_prev, adjoint_now, forward_snaps, courant, traces, rec_x, rec_y, water_rows, direction
):
    now = adjoint_now
    shots, cells_x, depth_cells, cells_y = now.shape
    parts = lax.axis_size("shot")
    bricks = lax.axis_size("brick")
    rows_part = depth_cells // parts
    columns = 4
    along = [[g + columns * i for i in range(bricks // columns)] for g in range(columns)]
    across = [
        [bricks * s + columns * g + i for s in range(parts) for i in range(columns)]
        for g in range(bricks // columns)
    ]
    beside = [
        [bricks * (2 * c + core) + columns * g + i for core in range(2) for i in range(columns)]
        for c in range(parts // 2)
        for g in range(bricks // columns)
    ]
    shot = lax.axis_index("shot")
    first_row = (lax.axis_index("brick") * cells_x).astype(jnp.int32)[None]
    core = (shot % 2).astype(jnp.int32)[None]
    offset = (shot * rows_part).astype(jnp.int32)
    smem = pl.BlockSpec(memory_space=pltpu.SMEM)
    shape = jax.ShapeDtypeStruct
    halves_shape = shape((2, parts // 2, cells_x, rows_part, cells_y), f32)

    illum_halves = pl.pallas_call(
        illum_kernel,
        out_shape=halves_shape,
        in_specs=vmem(1) + [smem, smem, smem],
        out_specs=vmem(1)[0],
        compiler_params=params,
        cost_estimate=pl.CostEstimate(flops=10**6, bytes_accessed=2 * 10**6, transcendentals=0),
    )(forward_snaps, core, first_row, offset[None])
    illum_mine = illum_halves[0] + exchanged(illum_halves)
    illum_got = four_chips(illum_mine)

    illum_part, own_peak = pl.pallas_call(
        peak_kernel,
        out_shape=(
            shape((cells_x, rows_part, cells_y), f32),
            shape((len(along[0]), 1, 128), f32),
        ),
        in_specs=vmem(1),
        out_specs=tuple(vmem(2)),
        compiler_params=params,
        cost_estimate=pl.CostEstimate(flops=10**5, bytes_accessed=4 * 10**5, transcendentals=0),
    )(illum_got)
    peak = fan(jnp.maximum, swapped(own_peak, "brick", along), len(beside[0]))

    side_shape = shape((2 * shots + 1, 2, depth_cells, cells_y), f32)
    local = pl.pallas_call(
        local_kernel,
        out_shape=shape(now.shape, f32),
        in_specs=vmem(2),
        out_specs=vmem(1)[0],
        compiler_params=params,
        cost_estimate=pl.CostEstimate(flops=10**7, bytes_accessed=4 * 10**6, transcendentals=0),
    )(now, courant)
    head, tail, traces, rec_x, rec_y = pl.pallas_call(
        edges_kernel,
        out_shape=(
            side_shape,
            side_shape,
            shape(traces.shape, f32),
            shape(rec_x.shape, jnp.int32),
            shape(rec_y.shape, jnp.int32),
        ),
        in_specs=vmem(7),
        out_specs=tuple(vmem(5)),
        compiler_params=params,
        cost_estimate=pl.CostEstimate(flops=10**5, bytes_accessed=10**6, transcendentals=0),
    )(local, adjoint_prev, now, courant, traces, rec_x, rec_y)
    before = to_next(tail)
    after = to_previous(head)

    image_halves = pl.pallas_call(
        image_kernel,
        out_shape=halves_shape,
        in_specs=vmem(10) + [smem, smem] + vmem(1),
        out_specs=vmem(1)[0],
        scratch_shapes=[
            pltpu.VMEM((shots, cells_x + 4, depth_cells, cells_y), f32),
            pltpu.VMEM((shots, 2, cells_x + 8, cells_y), f32),
        ],
        compiler_params=params,
        cost_estimate=pl.CostEstimate(flops=10**7, bytes_accessed=6 * 10**6, transcendentals=0),
    )(
        local, adjoint_prev, now, courant, before, after, forward_snaps,
        traces, rec_x, rec_y, first_row, core, peak,
    )
    peaks = swapped(peak, ("shot", "brick"), beside)
    pieces = pl.pallas_call(
        join_kernel,
        out_shape=shape((parts // 2, cells_x + 1, rows_part, cells_y), f32),
        in_specs=vmem(3),
        out_specs=vmem(1)[0],
        compiler_params=params,
        cost_estimate=pl.CostEstimate(flops=10**5, bytes_accessed=10**6, transcendentals=0),
    )(image_halves, exchanged(image_halves), peaks)
    image_got = four_chips(pieces)

    gradient, sums = pl.pallas_call(
        gradient_kernel,
        out_shape=(shape((cells_x, rows_part, cells_y), f32), shape((len(across[0]), 1, 256), f32)),
        in_specs=vmem(4) + [smem],
        out_specs=tuple(vmem(2)),
        compiler_params=params,
        cost_estimate=pl.CostEstimate(flops=10**6, bytes_accessed=6 * 10**5, transcendentals=0),
    )(image_got, illum_part, water_rows, direction, offset[None])
    sums = fan(jnp.add, swapped(sums, ("shot", "brick"), across), len(along[0]))
    gradient, sums = pl.pallas_call(
        last_kernel,
        out_shape=(shape(gradient.shape, f32), shape((2,), f32)),
        in_specs=vmem(2),
        out_specs=(vmem(1)[0], smem),
        compiler_params=params,
        cost_estimate=pl.CostEstimate(flops=10**4, bytes_accessed=2 * 10**5, transcendentals=0),
    )(swapped(sums, "brick", along), gradient)
    return (gradient, sums)


def solution(mesh):
    in_specs = (
        P("shot", "brick", None, None),
        P("shot", "brick", None, None),
        P("shot", None, "brick", None, None),
        P("brick", None, None),
        P("shot", None, None),
        P("shot", None),
        P("shot", None),
        P("brick", None),
        P("brick", None, None),
    )
    out_specs = (P("brick", "shot", None), P())
    return jax.shard_map(
        per_device, mesh=mesh, in_specs=in_specs, out_specs=out_specs, check_vma=False
    )
```
